128 devices in a mesh: seg: 4 (over x_hi, core), ch: 32 (over z, y, x_lo).
Axes of the slice: x: 4 (x_hi: 2, x_lo: 2; x = x_hi * 2 + x_lo), y: 4, z: 4, core: 2. Of those that a mesh axis runs over, the one named last changes fastest.
Arguments:
- raw: bfloat16 [64, 4096, 1024], P('seg', 'ch')
- source_index: int32 [16], replicated, may hold values from 0 to 4095, as said below
- source_block: int32 [16], replicated, may hold values from 0 to 3, as said below
Outputs:
- stacked: float32 [4096, 16, 128], P(('ch', 'seg'))
The draws below stay inside these ranges and needn't reach their ends.
Inputs may be any that keep to these rules, and one draw needn't show every extreme that they name: `source_index`: the 16 channels are distinct. `source_block`: every block holds exactly 4 sources.
All inputs are finite; a program needn't handle non-finite values.
Results may differ from the reference program's by a relative error of at most 0.002.
Values may be sent and summed in bfloat16 or wider, within the bound.
No kernel may reach another device: no remote copies, remote signals or barrier semaphores. Data moves between devices by JAX's collectives and lax.ppermute only.
A program may use at most 64 MiB of HBM per device.

```python
import math
import jax
import jax.numpy as jnp
from jax import lax

SEGLEN = 1024
FREQS = 512
HALFLAG = 64
LAGS = 128
SMOOTH = 4
SOURCES = 16
BLOCKS = 4
PER_BLOCK = 4
CHANNELS = 4096
SEGMENTS = 64


def draw_raw(key, part):
    key = jax.random.fold_in(key, 11)
    key_series, key_noise = jax.random.split(key, 2)
    length = SEGMENTS * SEGLEN + CHANNELS // 4 + 1
    series = jax.random.normal(key_series, (length,), jnp.float32)
    shape = (SEGMENTS, CHANNELS, SEGLEN)
    where = lax.broadcasted_iota(jnp.int32, shape, 0) * SEGLEN + lax.broadcasted_iota(jnp.int32, shape, 2) + lax.broadcasted_iota(jnp.int32, shape, 1) // 4
    coherent = series[where]
    noise = jax.random.normal(key_noise, shape, jnp.float32)
    value = 0.8 * coherent + noise
    return value.astype(jnp.bfloat16)


def draw_source_index(key, part):
    key = jax.random.fold_in(key, 12)
    return jax.random.permutation(key, CHANNELS)[:SOURCES].astype(jnp.int32)


def draw_source_block(key, part):
    key = jax.random.fold_in(key, 13)
    order = jax.random.permutation(key, SOURCES).astype(jnp.int32)
    return (order % BLOCKS).astype(jnp.int32)


def setup_inputs(seed: int = 0) -> dict:
    streams_of = jax.random.split(jax.random.key(seed), 4)
    raw = draw_raw(jax.random.fold_in(streams_of[3], 71), 0)
    source_index = draw_source_index(jax.random.fold_in(streams_of[3], 71), 0)
    source_block = draw_source_block(jax.random.fold_in(streams_of[3], 71), 0)
    return dict(raw=raw, source_index=source_index, source_block=source_block)


WATER = 0.1
EPS = 1e-06

def dft_table(length, count):
    times = lax.broadcasted_iota(jnp.int32, (length, count), 0)
    bins = lax.broadcasted_iota(jnp.int32, (length, count), 1) + 1
    phase = (bins * times % length).astype(jnp.float32) * (2.0 * math.pi / length)
    return jnp.concatenate([jnp.cos(phase), -jnp.sin(phase)], axis=1).astype(jnp.bfloat16)

def lag_tables(count, length, half):
    bins = lax.broadcasted_iota(jnp.int32, (count, 2 * half), 0) + 1
    shifts = lax.broadcasted_iota(jnp.int32, (count, 2 * half), 1) - half
    theta = (bins * shifts % length).astype(jnp.float32) * (2.0 * math.pi / length)
    return (jnp.cos(theta), jnp.sin(theta))

def whiten_rows(spectrum, count, half):
    real = spectrum[:, :count]
    imag = spectrum[:, count:]
    amplitude = jnp.sqrt(real * real + imag * imag)
    padded = jnp.pad(amplitude, ((0, 0), (half, half)))
    smoothed = padded[:, 0:count]
    for shift in range(1, 2 * half + 1):
        smoothed = smoothed + padded[:, shift:shift + count]
    smoothed = smoothed / (2 * half + 1)
    level = lax.optimization_barrier(jnp.mean(amplitude, axis=1, keepdims=True))
    divisor = smoothed + WATER * level + EPS
    return (spectrum / jnp.concatenate([divisor, divisor], axis=1)).astype(jnp.bfloat16)

def slot_channels(source_index, source_block, per_block):
    count = source_index.shape[0]
    later = lax.broadcasted_iota(jnp.int32, (count, count), 0) > lax.broadcasted_iota(jnp.int32, (count, count), 1)
    same = source_block[:, None] == source_block[None, :]
    rank = lax.optimization_barrier(jnp.sum(jnp.where(later & same, 1, 0), axis=1)).astype(jnp.int32)
    slot = source_block * per_block + rank
    place = slot[None, :] == lax.broadcasted_iota(jnp.int32, (count, count), 0)
    return lax.optimization_barrier(jnp.sum(jnp.where(place, source_index[None, :], 0), axis=1)).astype(jnp.int32)

def build_kernel(spec, cos_table, sin_table, count):
    real = spec[:, :count][:, :, None]
    imag = spec[:, count:][:, :, None]
    real_part = real * cos_table[None] - imag * sin_table[None]
    imag_part = real * sin_table[None] + imag * cos_table[None]
    joined = jnp.concatenate([real_part, imag_part], axis=1)
    width = joined.shape[0] * joined.shape[2]
    return jnp.transpose(joined, (1, 0, 2)).reshape(2 * count, width).astype(jnp.bfloat16)

def reference(raw, source_index, source_block):
    table = dft_table(SEGLEN, FREQS).astype(jnp.float32)
    cos_table, sin_table = lag_tables(FREQS, SEGLEN, HALFLAG)
    slot_channel = slot_channels(source_index, source_block, PER_BLOCK)
    scale = 1.0 / (FREQS * SEGMENTS)

    def one_segment(total, segment):
        spectrum = jnp.dot(segment.astype(jnp.float32), table, precision=lax.Precision.HIGHEST)
        whitened = whiten_rows(spectrum, FREQS, SMOOTH)
        source_spec = whitened[slot_channel].astype(jnp.float32)
        kernel = build_kernel(source_spec, cos_table, sin_table, FREQS)
        term = jnp.dot(whitened.astype(jnp.float32), kernel.astype(jnp.float32), precision=lax.Precision.HIGHEST)
        return (total + term * scale, None)
    start = jnp.zeros((CHANNELS, SOURCES * LAGS), jnp.float32)
    total, unused = lax.scan(one_segment, start, raw)
    return total.reshape(CHANNELS, SOURCES, LAGS)
```

```python
import jax
import jax.numpy as jnp
import ml_dtypes
import numpy as np
from jax import lax
from jax.experimental import pallas as pl
from jax.experimental.pallas import tpu as pltpu
from jax.sharding import PartitionSpec as P

SEGLEN = 1024
FREQS = 512
HALFLAG = 64
LAGS = 128
SMOOTH = 4
SOURCES = 16
PER_BLOCK = 4
WATER = 0.1
EPS = 1e-06

GROUPS = FREQS // 8
MIB = 1 << 20


def dft_rows():
    bins = np.arange(1, FREQS + 1)[:, None]
    times = np.arange(SEGLEN)[None, :]
    phase = ((bins * times) % SEGLEN).astype(np.float32) * np.float32(2.0 * np.pi / SEGLEN)
    table = np.concatenate([np.cos(phase), -np.sin(phase)], axis=0)
    return table.astype(ml_dtypes.bfloat16)


def lag_rows(scale):
    bins = np.arange(1, FREQS + 1)[None, :]
    lags = np.arange(LAGS)[:, None] - HALFLAG
    theta = ((bins * lags) % SEGLEN).astype(np.float32) * np.float32(2.0 * np.pi / SEGLEN)
    cos = np.cos(theta).reshape(LAGS, GROUPS, 1, 8)
    sin = np.sin(theta).reshape(LAGS, GROUPS, 1, 8)
    table = np.concatenate([cos, sin], axis=2).reshape(LAGS, 2 * FREQS) * np.float32(scale)
    high = table.astype(ml_dtypes.bfloat16)
    low = (table - high.astype(np.float32)).astype(ml_dtypes.bfloat16)
    return np.concatenate([high, low], axis=0)


def nt_dot(a, b):
    return lax.dot_general(a, b, (((1,), (1,)), ((), ())), preferred_element_type=jnp.float32)


def nn_dot(a, b):
    return lax.dot_general(a, b, (((1,), (0,)), ((), ())), preferred_element_type=jnp.float32)


def pick_body(index_ref, block_ref, raw_ref, out_ref, chan_ref, sel_ref):
    count = raw_ref.shape[1]

    @pl.when(pl.program_id(0) == 0)
    def _():
        first = lax.axis_index("ch") * count
        for s in range(SOURCES):
            rank = jnp.int32(0)
            for t in range(s):
                rank += jnp.where(block_ref[t] == block_ref[s], 1, 0).astype(jnp.int32)
            chan_ref[block_ref[s] * PER_BLOCK + rank] = index_ref[s] - first
        lane = lax.broadcasted_iota(jnp.int32, (8, count), 1)
        sub = lax.broadcasted_iota(jnp.int32, (8, count), 0)
        for q in range(SOURCES):
            hit = jnp.where(lane == chan_ref[q], 1.0, 0.0)
            for g in range(8):
                sel_ref[q * 8 : q * 8 + 8, g * count : (g + 1) * count] = jnp.where(sub == g, hit, 0.0)

    rows = raw_ref[...].reshape(8 * count, SEGLEN)
    got = nn_dot(sel_ref[...].astype(jnp.bfloat16), rows)
    out_ref[...] = got.astype(jnp.bfloat16).reshape(SOURCES, 1, 8, SEGLEN)


def pick(raw, source_index, source_block):
    segs, count, length = raw.shape
    return pl.pallas_call(
        pick_body,
        grid=(segs // 8,),
        in_specs=[
            pl.BlockSpec(memory_space=pltpu.SMEM),
            pl.BlockSpec(memory_space=pltpu.SMEM),
            pl.BlockSpec((8, count, length), lambda i: (i, 0, 0)),
        ],
        out_specs=pl.BlockSpec((SOURCES, 1, 8, length), lambda i: (0, i, 0, 0)),
        out_shape=jax.ShapeDtypeStruct((SOURCES, segs // 8, 8, length), jnp.bfloat16),
        scratch_shapes=[
            pltpu.SMEM((SOURCES,), jnp.int32),
            pltpu.VMEM((SOURCES * 8, 8 * count), jnp.float32),
        ],
        compiler_params=pltpu.CompilerParams(vmem_limit_bytes=32 * MIB),
        cost_estimate=pl.CostEstimate(flops=2 * 10**8, bytes_accessed=5 * 10**6, transcendentals=0),
        name="pick",
    )(source_index, source_block, raw)


def source_body(parts_ref, table_ref, out_ref):
    total = jnp.sum(parts_ref[...].astype(jnp.float32), axis=0)
    spectrum = nt_dot(total.astype(jnp.bfloat16), table_ref[...])
    real = spectrum[:, :FREQS]
    imag = spectrum[:, FREQS:]
    amplitude = jnp.sqrt(real * real + imag * imag)
    place = lax.broadcasted_iota(jnp.int32, amplitude.shape, 1)
    smoothed = amplitude
    for shift in range(1, SMOOTH + 1):
        later = pltpu.roll(amplitude, FREQS - shift, 1)
        smoothed += jnp.where(place < FREQS - shift, later, 0.0)
        earlier = pltpu.roll(amplitude, shift, 1)
        smoothed += jnp.where(place >= shift, earlier, 0.0)
    level = jnp.sum(amplitude, axis=1, keepdims=True) * (1.0 / FREQS)
    divisor = smoothed / (2 * SMOOTH + 1) + WATER * level + EPS
    real = (real / divisor).astype(jnp.bfloat16).astype(jnp.float32)
    imag = (imag / divisor).astype(jnp.bfloat16).astype(jnp.float32)
    sub = lax.broadcasted_iota(jnp.int32, (8, 128), 0)
    lane = lax.broadcasted_iota(jnp.int32, (8, 128), 1)
    block = (lane // 8) % 8

    def turn(x):
        for s in (4, 2, 1):
            down = pltpu.roll(pltpu.roll(x, s, 0), 128 - 8 * s, 1)
            up = pltpu.roll(pltpu.roll(x, 8 - s, 0), 8 * s, 1)
            low_row = (sub & s) == 0
            low_block = (block & s) == 0
            x = jnp.where(low_row == low_block, x, jnp.where(low_row, up, down))
        return x

    rows = []
    for j in range(FREQS // 128):
        re = turn(real[:, j * 128 : (j + 1) * 128])
        im = turn(imag[:, j * 128 : (j + 1) * 128])
        rows.append(jnp.where(lane < 64, re, pltpu.roll(im, 64, 1)))
        rows.append(jnp.where(lane < 64, pltpu.roll(re, 64, 1), im))
    packed = jnp.concatenate(rows, axis=0).astype(jnp.bfloat16)
    out_ref[...] = jnp.broadcast_to(packed[None], out_ref.shape)


def source_rows(parts, table):
    return pl.pallas_call(
        source_body,
        out_shape=jax.ShapeDtypeStruct((parts.shape[0], GROUPS, 128), jnp.bfloat16),
        in_specs=[pl.BlockSpec(memory_space=pltpu.VMEM)] * 2,
        out_specs=pl.BlockSpec(memory_space=pltpu.VMEM),
        compiler_params=pltpu.CompilerParams(vmem_limit_bytes=32 * MIB),
        cost_estimate=pl.CostEstimate(flops=2 * 8 * 1024 * 1024, bytes_accessed=3 * 10**6, transcendentals=0),
        name="source_rows",
    )(parts, table)


def whiten_body(raw_ref, table_ref, out_ref, spec_ref, amp_ref):
    width = raw_ref.shape[0] * raw_ref.shape[1]
    count = raw_ref.shape[1]
    rows = raw_ref[...].reshape(width, SEGLEN)
    spec_ref[...] = nt_dot(table_ref[...], rows)
    zero = jnp.zeros((8, width), jnp.float32)
    amp_ref[0:8, :] = zero
    amp_ref[FREQS + 8 : FREQS + 16, :] = zero
    step = 32
    level = zero
    for f in range(0, FREQS, step):
        real = spec_ref[f : f + step, :]
        imag = spec_ref[FREQS + f : FREQS + f + step, :]
        amplitude = jnp.sqrt(real * real + imag * imag)
        amp_ref[8 + f : 8 + f + step, :] = amplitude
        for i in range(0, step, 8):
            level += amplitude[i : i + 8]
    level = jnp.sum(level, axis=0, keepdims=True) * (WATER / FREQS) + EPS
    for f in range(0, FREQS, step):
        size = step + 16
        a = amp_ref[f : f + size, :]
        s2 = a + pltpu.roll(a, size - 1, 0)
        s4 = s2 + pltpu.roll(s2, size - 2, 0)
        s9 = s4 + pltpu.roll(s4, 4, 0) + pltpu.roll(a, size - 4, 0)
        inverse = 1.0 / (s9[8 : 8 + step] * (1.0 / (2 * SMOOTH + 1)) + level)
        real = spec_ref[f : f + step, :] * inverse
        imag = spec_ref[FREQS + f : FREQS + f + step, :] * inverse
        for part, value in ((0, real), (1, imag)):
            for i in range(0, step, 8):
                pair = jnp.concatenate(
                    [value[i : i + 8, :count], value[i : i + 8, count:]], axis=0
                )
                out_ref[(f + i) // 8, part, 0] = pair.astype(jnp.bfloat16)


def whiten(raw, table, half):
    segs, count, length = raw.shape
    pairs = segs // 4
    out = pl.pallas_call(
        whiten_body,
        grid=(pairs,),
        in_specs=[
            pl.BlockSpec((2, count, length), lambda i: (i + half * pairs, 0, 0)),
            pl.BlockSpec((2 * FREQS, length), lambda i: (0, 0)),
        ],
        out_specs=pl.BlockSpec((GROUPS, 2, 1, 16, count), lambda i: (0, 0, i, 0, 0)),
        out_shape=jax.ShapeDtypeStruct((GROUPS, 2, pairs, 16, count), jnp.bfloat16),
        scratch_shapes=[
            pltpu.VMEM((2 * FREQS, 2 * count), jnp.float32),
            pltpu.VMEM((FREQS + 16, 2 * count), jnp.float32),
        ],
        compiler_params=pltpu.CompilerParams(vmem_limit_bytes=32 * MIB),
        cost_estimate=pl.CostEstimate(
            flops=2 * 1024 * 1024 * 1024, bytes_accessed=6 * 10**6, transcendentals=10**6
        ),
        name=f"whiten{half}",
    )(raw, table)
    return out.reshape(GROUPS, 32 * pairs, count)


def correlate_body(src_ref, w0_ref, w1_ref, lag_ref, mine_ref, core_ref, far0_ref, far1_ref, s_ref, high_ref, low_ref, sum_ref):
    step = pl.program_id(0)
    blocks = w0_ref.shape[0]
    count = w0_ref.shape[2]
    pairs = SOURCES // 2

    @pl.when(step == 0)
    def _():
        lane = lax.broadcasted_iota(jnp.int32, (GROUPS, 128), 1)
        for i in range(2 * SOURCES):
            value = src_ref[i].astype(jnp.float32)
            s_ref[0, i] = value
            turned = pltpu.roll(value, 64, 1)
            s_ref[1, i] = jnp.where(lane < 64, -turned, turned)

    sub = lax.broadcasted_iota(jnp.int32, (8, 128), 0)
    lane = lax.broadcasted_iota(jnp.int32, (8, 128), 1)
    diagonal = (lane % 8) == sub
    for j in range(blocks):
        b = step * blocks + j
        tiles = []
        for q in range(SOURCES):
            halves = []
            for h in range(2):
                parts = []
                for r in range(2):
                    row = jnp.broadcast_to(s_ref[r, 2 * q + h, pl.ds(b, 1), :], (8, 128))
                    parts.append(jnp.where(diagonal, row, 0.0))
                halves.append(jnp.concatenate(parts, axis=0).astype(jnp.bfloat16))
            tiles.append(jnp.concatenate(halves, axis=1))
        left = jnp.concatenate(tiles, axis=0)
        right = jnp.concatenate([w0_ref[j], w1_ref[j]], axis=0)
        cross = nn_dot(left, right)
        high = cross.astype(jnp.bfloat16)
        low = (cross - high.astype(jnp.float32)).astype(jnp.bfloat16)
        at = pl.ds(pl.multiple_of(b * 16, 16), 16)
        for q in range(SOURCES):
            cols = slice((q % 2) * count, (q % 2 + 1) * count)
            high_ref[q // 2, at, cols] = high[q * 16 : q * 16 + 16]
            low_ref[q // 2, at, cols] = low[q * 16 : q * 16 + 16]

    @pl.when(step == pl.num_programs(0) - 1)
    def _():
        me = lax.axis_index("seg")
        share = count // 4
        for p in range(pairs):
            first = nn_dot(lag_ref[...], high_ref[p])
            second = nn_dot(lag_ref[:LAGS, :], low_ref[p])
            total = first[:LAGS] + (first[LAGS:] + second)
            for i in range(2):
                sum_ref[2 * p + i] = total[:, i * count : (i + 1) * count].T

        def part(r):
            return sum_ref[:, pl.ds(pl.multiple_of((me ^ r) * share, share), share), :]

        mine_ref[...] = part(0)
        core_ref[...] = part(1)
        far0_ref[...] = part(2).astype(jnp.bfloat16)
        far1_ref[...] = part(3).astype(jnp.bfloat16)


def correlate(src, w0, w1, lag):
    count = w0.shape[2]
    blocks = 8
    share = count // 4
    shape = (SOURCES, share, LAGS)
    whole = pl.BlockSpec(shape, lambda i: (0, 0, 0))
    return pl.pallas_call(
        correlate_body,
        grid=(GROUPS // blocks,),
        in_specs=[
            pl.BlockSpec(src.shape, lambda i: (0, 0, 0)),
            pl.BlockSpec((blocks, 128, count), lambda i: (i, 0, 0)),
            pl.BlockSpec((blocks, 128, count), lambda i: (i, 0, 0)),
            pl.BlockSpec(lag.shape, lambda i: (0, 0)),
        ],
        out_specs=[whole] * 4,
        out_shape=[
            jax.ShapeDtypeStruct(shape, jnp.float32),
            jax.ShapeDtypeStruct(shape, jnp.float32),
            jax.ShapeDtypeStruct(shape, jnp.bfloat16),
            jax.ShapeDtypeStruct(shape, jnp.bfloat16),
        ],
        scratch_shapes=[
            pltpu.VMEM((2, 2 * SOURCES, GROUPS, 128), jnp.float32),
            pltpu.VMEM((SOURCES // 2, 2 * FREQS, 2 * count), jnp.bfloat16),
            pltpu.VMEM((SOURCES // 2, 2 * FREQS, 2 * count), jnp.bfloat16),
            pltpu.VMEM((SOURCES, count, LAGS), jnp.float32),
        ],
        compiler_params=pltpu.CompilerParams(vmem_limit_bytes=40 * MIB),
        cost_estimate=pl.CostEstimate(flops=3 * 10**9, bytes_accessed=6 * 10**6, transcendentals=0),
        name="correlate",
    )(src, w0, w1, lag)


def gather_sum_body(mine_ref, core_ref, far0_ref, far1_ref, out_ref):
    far = far0_ref[...].astype(jnp.float32) + far1_ref[...].astype(jnp.float32)
    total = (mine_ref[...] + core_ref[...]) + far
    for q in range(SOURCES):
        out_ref[:, q, :] = total[q]


def gather_sum(mine, core, far0, far1):
    shape = mine.shape
    return pl.pallas_call(
        gather_sum_body,
        in_specs=[pl.BlockSpec(memory_space=pltpu.VMEM)] * 4,
        out_specs=pl.BlockSpec(memory_space=pltpu.VMEM),
        out_shape=jax.ShapeDtypeStruct((shape[1], shape[0], shape[2]), jnp.float32),
        cost_estimate=pl.CostEstimate(flops=10**6, bytes_accessed=10**6, transcendentals=0),
        name="gather_sum",
    )(mine, core, far0, far1)


def local(raw, source_index, source_block):
    segs = raw.shape[0] * lax.axis_size("seg")
    ways = lax.axis_size("ch")
    table = jnp.asarray(dft_rows())
    lag = jnp.asarray(lag_rows(1.0 / (FREQS * segs)))
    picked = pick(raw, source_index, source_block).reshape(ways, 8, SEGLEN)
    parts = lax.all_to_all(picked, "ch", 0, 0)
    w0 = whiten(raw, table, 0)
    spread = source_rows(parts, table)
    src = lax.all_to_all(spread, "ch", 0, 0)
    w1 = whiten(raw, table, 1)
    mine, core, far0, far1 = correlate(src, w0, w1, lag)

    def swap(x, r):
        return lax.ppermute(x, "seg", [(i, i ^ r) for i in range(4)])

    return gather_sum(mine, swap(core, 1), swap(far0, 2), swap(far1, 3))


def solution(mesh):
    return jax.shard_map(
        local,
        mesh=mesh,
        in_specs=(P("seg", "ch", None), P(), P()),
        out_specs=P(("ch", "seg"), None, None),
        check_vma=False,
    )
```

```python
import functools

import jax
import jax.numpy as jnp
import ml_dtypes
import numpy as np
from jax import lax
from jax.experimental import pallas as pl
from jax.experimental.pallas import tpu as pltpu
from jax.sharding import PartitionSpec as P

SEGLEN = 1024
FREQS = 512
HALFLAG = 64
LAGS = 128
SMOOTH = 4
SOURCES = 16
PER_BLOCK = 4
WATER = 0.1
EPS = 1e-06

GROUPS = FREQS // 8
PICK_VMEM = 58 << 20
WHITEN_VMEM = 52 << 20
SOURCE_VMEM = 48 << 20
CORRELATE_VMEM = 52 << 20
SUM_VMEM = 14 << 20


def dft_rows():
    bins = np.arange(1, FREQS + 1)[:, None]
    times = np.arange(SEGLEN)[None, :]
    phase = ((bins * times) % SEGLEN).astype(np.float32) * np.float32(2.0 * np.pi / SEGLEN)
    table = np.concatenate([np.cos(phase), -np.sin(phase)], axis=0)
    return table.astype(ml_dtypes.bfloat16)


def lag_rows(scale):
    bins = np.arange(1, FREQS + 1)[None, :]
    lags = np.arange(LAGS)[:, None] - HALFLAG
    theta = ((bins * lags) % SEGLEN).astype(np.float32) * np.float32(2.0 * np.pi / SEGLEN)
    cos = np.cos(theta).reshape(LAGS, GROUPS, 1, 8)
    sin = np.sin(theta).reshape(LAGS, GROUPS, 1, 8)
    table = np.concatenate([cos, sin], axis=2).reshape(LAGS, 2 * FREQS) * np.float32(scale)
    high = table.astype(ml_dtypes.bfloat16)
    low = (table - high.astype(np.float32)).astype(ml_dtypes.bfloat16)
    return np.concatenate([high, low], axis=0)


def nt_dot(a, b):
    return lax.dot_general(a, b, (((1,), (1,)), ((), ())), preferred_element_type=jnp.float32)


def nn_dot(a, b):
    return lax.dot_general(a, b, (((1,), (0,)), ((), ())), preferred_element_type=jnp.float32)


def pick_body(index_ref, block_ref, raw_ref, out_ref, chan_ref, sel_ref, held_ref, sems):
    segs, count, _ = raw_ref.shape
    copies = []
    for i in range(segs // 2):
        part = pl.ds(2 * i, 2)
        copies.append(pltpu.make_async_copy(raw_ref.at[part], held_ref.at[part], sems.at[i]))
        copies[-1].start()
    first = lax.axis_index("ch") * count
    for s in range(SOURCES):
        rank = jnp.int32(0)
        for t in range(s):
            rank += jnp.where(block_ref[t] == block_ref[s], 1, 0).astype(jnp.int32)
        chan_ref[block_ref[s] * PER_BLOCK + rank] = index_ref[s] - first
    lane = lax.broadcasted_iota(jnp.int32, (8, count), 1)
    sub = lax.broadcasted_iota(jnp.int32, (8, count), 0)
    for q in range(SOURCES):
        hit = jnp.where(lane == chan_ref[q], 1.0, 0.0)
        for g in range(8):
            sel_ref[q * 8 : q * 8 + 8, g * count : (g + 1) * count] = jnp.where(sub == g, hit, 0.0)
    select = sel_ref[...].astype(jnp.bfloat16)
    for h in range(segs // 8):
        for i in range(4 * h, 4 * h + 4):
            copies[i].wait()
        rows = held_ref[8 * h : 8 * h + 8].reshape(8 * count, SEGLEN)
        out_ref[:, h] = nn_dot(select, rows).astype(jnp.bfloat16).reshape(SOURCES, 8, SEGLEN)


def pick(raw, source_index, source_block):
    segs, count, length = raw.shape
    return pl.pallas_call(
        pick_body,
        grid_spec=pltpu.PrefetchScalarGridSpec(
            num_scalar_prefetch=2,
            grid=(1,),
            in_specs=[pl.BlockSpec(memory_space=pl.ANY)],
            out_specs=pl.BlockSpec((SOURCES, segs // 8, 8, length), lambda i, *_: (0, 0, 0, 0)),
            scratch_shapes=[
                pltpu.SMEM((SOURCES,), jnp.int32),
                pltpu.VMEM((SOURCES * 8, 8 * count), jnp.float32),
                pltpu.VMEM(raw.shape, raw.dtype),
                pltpu.SemaphoreType.DMA((segs // 2,)),
            ],
        ),
        out_shape=jax.ShapeDtypeStruct((SOURCES, segs // 8, 8, length), jnp.bfloat16),
        compiler_params=pltpu.CompilerParams(vmem_limit_bytes=PICK_VMEM),
        cost_estimate=pl.CostEstimate(flops=2 * 10**8, bytes_accessed=5 * 10**6, transcendentals=0),
        name="pick",
    )(source_index, source_block, raw)


def source_body(parts_ref, table_ref, after_ref, out_ref):
    total = jnp.sum(parts_ref[...].astype(jnp.float32), axis=0)
    spectrum = nt_dot(total.astype(jnp.bfloat16), table_ref[...])
    real = spectrum[:, :FREQS]
    imag = spectrum[:, FREQS:]
    amplitude = jnp.sqrt(real * real + imag * imag)
    place = lax.broadcasted_iota(jnp.int32, amplitude.shape, 1)
    smoothed = amplitude
    for shift in range(1, SMOOTH + 1):
        later = pltpu.roll(amplitude, FREQS - shift, 1)
        smoothed += jnp.where(place < FREQS - shift, later, 0.0)
        earlier = pltpu.roll(amplitude, shift, 1)
        smoothed += jnp.where(place >= shift, earlier, 0.0)
    level = jnp.sum(amplitude, axis=1, keepdims=True) * (1.0 / FREQS)
    divisor = smoothed / (2 * SMOOTH + 1) + WATER * level + EPS
    real = (real / divisor).astype(jnp.bfloat16).astype(jnp.float32)
    imag = (imag / divisor).astype(jnp.bfloat16).astype(jnp.float32)
    sub = lax.broadcasted_iota(jnp.int32, (8, 128), 0)
    lane = lax.broadcasted_iota(jnp.int32, (8, 128), 1)
    block = (lane // 8) % 8

    def turn(x):
        for s in (4, 2, 1):
            down = pltpu.roll(pltpu.roll(x, s, 0), 128 - 8 * s, 1)
            up = pltpu.roll(pltpu.roll(x, 8 - s, 0), 8 * s, 1)
            low_row = (sub & s) == 0
            low_block = (block & s) == 0
            x = jnp.where(low_row == low_block, x, jnp.where(low_row, up, down))
        return x

    rows = []
    for j in range(FREQS // 128):
        re = turn(real[:, j * 128 : (j + 1) * 128])
        im = turn(imag[:, j * 128 : (j + 1) * 128])
        rows.append(jnp.where(lane < 64, re, pltpu.roll(im, 64, 1)))
        rows.append(jnp.where(lane < 64, pltpu.roll(re, 64, 1), im))
    packed = jnp.concatenate(rows, axis=0).astype(jnp.bfloat16)
    out_ref[...] = jnp.broadcast_to(packed[None], out_ref.shape)


def source_rows(parts, table, after):
    return pl.pallas_call(
        source_body,
        out_shape=jax.ShapeDtypeStruct((parts.shape[0], GROUPS, 128), jnp.bfloat16),
        in_specs=[pl.BlockSpec(memory_space=pltpu.VMEM)] * 2 + [pl.BlockSpec(memory_space=pl.ANY)],
        out_specs=pl.BlockSpec(memory_space=pltpu.VMEM),
        compiler_params=pltpu.CompilerParams(vmem_limit_bytes=SOURCE_VMEM),
        cost_estimate=pl.CostEstimate(flops=2 * 8 * 1024 * 1024, bytes_accessed=3 * 10**6, transcendentals=0),
        name="source_rows",
    )(parts, table, after)


def whiten_body(raw_ref, table_ref, out_ref, done_ref, spec_ref, amp_ref):
    count = raw_ref.shape[1]
    width = 2 * count
    step = 32
    size = step + 16
    zero = jnp.zeros((8, width), jnp.float32)
    done_ref[...] = zero[:, :128]
    amp_ref[0:8, :] = zero
    amp_ref[FREQS + 8 : FREQS + 16, :] = zero
    spec_ref[...] = nt_dot(table_ref[...], raw_ref[...].reshape(width, SEGLEN))
    level = zero
    for f in range(0, FREQS, step):
        real = spec_ref[f : f + step, :]
        imag = spec_ref[FREQS + f : FREQS + f + step, :]
        amplitude = jnp.sqrt(real * real + imag * imag)
        amp_ref[8 + f : 8 + f + step, :] = amplitude
        for i in range(0, step, 8):
            level += amplitude[i : i + 8]
    level = jnp.sum(level, axis=0, keepdims=True) * (WATER / FREQS) + EPS
    for f in range(0, FREQS, step):
        a = amp_ref[f : f + size, :]
        s2 = a + pltpu.roll(a, size - 1, 0)
        s4 = s2 + pltpu.roll(s2, size - 2, 0)
        s9 = s4 + pltpu.roll(s4, 4, 0) + pltpu.roll(a, size - 4, 0)
        inverse = 1.0 / (s9[8 : 8 + step] * (1.0 / (2 * SMOOTH + 1)) + level)
        real = spec_ref[f : f + step, :] * inverse
        imag = spec_ref[FREQS + f : FREQS + f + step, :] * inverse
        for part, value in ((0, real), (1, imag)):
            for i in range(0, step, 8):
                both = jnp.concatenate([value[i : i + 8, :count], value[i : i + 8, count:]], axis=0)
                out_ref[(f + i) // 8, part, 0] = both.astype(jnp.bfloat16)


def whiten(raw, table, half):
    segs, count, length = raw.shape
    pairs = segs // 4
    out, done = pl.pallas_call(
        whiten_body,
        grid=(pairs,),
        in_specs=[
            pl.BlockSpec((2, count, length), lambda i: (i + half * pairs, 0, 0)),
            pl.BlockSpec((2 * FREQS, length), lambda i: (0, 0)),
        ],
        out_specs=[
            pl.BlockSpec((GROUPS, 2, 1, 16, count), lambda i: (0, 0, i, 0, 0)),
            pl.BlockSpec((8, 128), lambda i: (0, 0)),
        ],
        out_shape=[
            jax.ShapeDtypeStruct((GROUPS, 2, pairs, 16, count), jnp.bfloat16),
            jax.ShapeDtypeStruct((8, 128), jnp.float32),
        ],
        scratch_shapes=[
            pltpu.VMEM((2 * FREQS, 2 * count), jnp.float32),
            pltpu.VMEM((FREQS + 16, 2 * count), jnp.float32),
        ],
        compiler_params=pltpu.CompilerParams(vmem_limit_bytes=WHITEN_VMEM),
        cost_estimate=pl.CostEstimate(
            flops=2 * 1024 * 1024 * 1024, bytes_accessed=6 * 10**6, transcendentals=10**6
        ),
        name=f"whiten{half}",
    )(raw, table)
    return out.reshape(GROUPS, 32 * pairs, count), done


def correlate_body(
    src_ref, w0_ref, w1_ref, lag_ref, mine_ref, core_ref, far0_ref, far1_ref,
    s_ref, w_ref, table_ref, high_ref, low_ref, sum_ref, sems, table_sem,
):
    count = w0_ref.shape[2]
    deep = w0_ref.shape[1]
    parts = sems.shape[0]
    blocks = GROUPS // parts

    def load(i, half):
        at = pl.ds(i * blocks, blocks)
        source = (w0_ref, w1_ref)[half]
        return pltpu.make_async_copy(
            source.at[at], w_ref.at[at, pl.ds(half * deep, deep)], sems.at[i, half]
        )

    for i in range(parts):
        load(i, 0).start()
        load(i, 1).start()
    table_copy = pltpu.make_async_copy(lag_ref, table_ref, table_sem)
    table_copy.start()

    lanes = lax.broadcasted_iota(jnp.int32, (GROUPS, 128), 1)
    for i in range(2 * SOURCES):
        value = src_ref[i].astype(jnp.float32)
        s_ref[0, i] = value
        turned = pltpu.roll(value, 64, 1)
        s_ref[1, i] = jnp.where(lanes < 64, -turned, turned)

    sub = lax.broadcasted_iota(jnp.int32, (8, 128), 0)
    lane = lax.broadcasted_iota(jnp.int32, (8, 128), 1)
    diagonal = (lane % 8) == sub

    def chunk(i, carry):
        load(i, 0).wait()
        load(i, 1).wait()
        for j in range(blocks):
            b = i * blocks + j
            tiles = []
            for q in range(SOURCES):
                halves = []
                for h in range(2):
                    pieces = []
                    for r in range(2):
                        row = jnp.broadcast_to(s_ref[r, 2 * q + h, pl.ds(b, 1), :], (8, 128))
                        pieces.append(jnp.where(diagonal, row, 0.0))
                    halves.append(jnp.concatenate(pieces, axis=0).astype(jnp.bfloat16))
                tiles.append(jnp.concatenate(halves, axis=1))
            cross = nn_dot(jnp.concatenate(tiles, axis=0), w_ref[b])
            high = cross.astype(jnp.bfloat16)
            low = (cross - high.astype(jnp.float32)).astype(jnp.bfloat16)
            at = pl.ds(pl.multiple_of(b * 16, 16), 16)
            for q in range(SOURCES):
                cols = slice((q % 2) * count, (q % 2 + 1) * count)
                high_ref[q // 2, at, cols] = high[q * 16 : q * 16 + 16]
                low_ref[q // 2, at, cols] = low[q * 16 : q * 16 + 16]
        return carry

    lax.fori_loop(0, parts, chunk, 0)
    table_copy.wait()
    me = lax.axis_index("seg")
    share = count // 4
    for p in range(SOURCES // 2):
        first = nn_dot(table_ref[...], high_ref[p])
        second = nn_dot(table_ref[:LAGS, :], low_ref[p])
        total = first[:LAGS] + (first[LAGS:] + second)
        for i in range(2):
            sum_ref[2 * p + i] = total[:, i * count : (i + 1) * count].T

    def part(r):
        return sum_ref[:, pl.ds(pl.multiple_of((me ^ r) * share, share), share), :]

    mine_ref[...] = part(0)
    core_ref[...] = part(1)
    far0_ref[...] = part(2).astype(jnp.bfloat16)
    far1_ref[...] = part(3).astype(jnp.bfloat16)


def correlate(src, w0, w1, lag):
    count = w0.shape[2]
    parts = 8
    share = count // 4
    shape = (SOURCES, share, LAGS)
    vmem = pl.BlockSpec(memory_space=pltpu.VMEM)
    anywhere = pl.BlockSpec(memory_space=pl.ANY)
    return pl.pallas_call(
        correlate_body,
        in_specs=[vmem, anywhere, anywhere, anywhere],
        out_specs=[vmem] * 4,
        out_shape=[
            jax.ShapeDtypeStruct(shape, jnp.float32),
            jax.ShapeDtypeStruct(shape, jnp.float32),
            jax.ShapeDtypeStruct(shape, jnp.bfloat16),
            jax.ShapeDtypeStruct(shape, jnp.bfloat16),
        ],
        scratch_shapes=[
            pltpu.VMEM((2, 2 * SOURCES, GROUPS, 128), jnp.float32),
            pltpu.VMEM((GROUPS, 2 * w0.shape[1], count), jnp.bfloat16),
            pltpu.VMEM(lag.shape, lag.dtype),
            pltpu.VMEM((SOURCES // 2, 2 * FREQS, 2 * count), jnp.bfloat16),
            pltpu.VMEM((SOURCES // 2, 2 * FREQS, 2 * count), jnp.bfloat16),
            pltpu.VMEM((SOURCES, count, LAGS), jnp.float32),
            pltpu.SemaphoreType.DMA((parts, 2)),
            pltpu.SemaphoreType.DMA,
        ],
        compiler_params=pltpu.CompilerParams(vmem_limit_bytes=CORRELATE_VMEM),
        cost_estimate=pl.CostEstimate(flops=3 * 10**9, bytes_accessed=6 * 10**6, transcendentals=0),
        name="correlate",
    )(src, w0, w1, lag)


def gather_sum_body(mine_ref, core_ref, far0_ref, far1_ref, out_ref):
    far = far0_ref[...].astype(jnp.float32) + far1_ref[...].astype(jnp.float32)
    total = (mine_ref[...] + core_ref[...]) + far
    for q in range(SOURCES):
        out_ref[:, q, :] = total[q]


def gather_sum(mine, core, far0, far1):
    shape = mine.shape
    return pl.pallas_call(
        gather_sum_body,
        in_specs=[pl.BlockSpec(memory_space=pltpu.VMEM)] * 4,
        out_specs=pl.BlockSpec(memory_space=pltpu.VMEM),
        out_shape=jax.ShapeDtypeStruct((shape[1], shape[0], shape[2]), jnp.float32),
        compiler_params=pltpu.CompilerParams(vmem_limit_bytes=SUM_VMEM),
        cost_estimate=pl.CostEstimate(flops=10**6, bytes_accessed=10**6, transcendentals=0),
        name="gather_sum",
    )(mine, core, far0, far1)


def local(raw, source_index, source_block):
    segs = raw.shape[0] * lax.axis_size("seg")
    ways = lax.axis_size("ch")
    table = jnp.asarray(dft_rows())
    lag = jnp.asarray(lag_rows(1.0 / (FREQS * segs)))
    picked = pick(raw, source_index, source_block)
    parts = lax.all_to_all(picked.reshape(ways, 8, SEGLEN), "ch", 0, 0)
    w0, done = whiten(raw, table, 0)
    spread = source_rows(parts, table, done)
    src = lax.all_to_all(spread, "ch", 0, 0)
    w1, _ = whiten(raw, table, 1)
    mine, core, far0, far1 = correlate(src, w0, w1, lag)

    def swap(x, r):
        return lax.ppermute(x, "seg", [(i, i ^ r) for i in range(4)])

    return gather_sum(mine, swap(core, 1), swap(far0, 2), swap(far1, 3))


def solution(mesh):
    return jax.shard_map(
        local,
        mesh=mesh,
        in_specs=(P("seg", "ch", None), P(), P()),
        out_specs=P(("ch", "seg"), None, None),
        check_vma=False,
    )
```

```python
import functools

import jax
import jax.numpy as jnp
import ml_dtypes
import numpy as np
from jax import lax
from jax.experimental import pallas as pl
from jax.experimental.pallas import tpu as pltpu
from jax.sharding import PartitionSpec as P

SEGLEN = 1024
FREQS = 512
HALFLAG = 64
LAGS = 128
SMOOTH = 4
SOURCES = 16
PER_BLOCK = 4
WATER = 0.1
EPS = 1e-06

GROUPS = FREQS // 8
PICK_VMEM = 58 << 20
WHITEN_VMEM = 52 << 20
SOURCE_VMEM = 48 << 20
CORRELATE_VMEM = 52 << 20
SUM_VMEM = 14 << 20


def dft_rows():
    bins = np.arange(1, FREQS + 1)[:, None]
    times = np.arange(SEGLEN)[None, :]
    phase = ((bins * times) % SEGLEN).astype(np.float32) * np.float32(2.0 * np.pi / SEGLEN)
    table = np.concatenate([np.cos(phase), -np.sin(phase)], axis=0)
    return table.astype(ml_dtypes.bfloat16)


def lag_rows(scale):
    bins = np.arange(1, FREQS + 1)[None, :]
    lags = np.arange(LAGS)[:, None] - HALFLAG
    theta = ((bins * lags) % SEGLEN).astype(np.float32) * np.float32(2.0 * np.pi / SEGLEN)
    cos = np.cos(theta).reshape(LAGS, GROUPS, 1, 8)
    sin = np.sin(theta).reshape(LAGS, GROUPS, 1, 8)
    table = np.concatenate([cos, sin], axis=2).reshape(LAGS, 2 * FREQS) * np.float32(scale)
    high = table.astype(ml_dtypes.bfloat16)
    low = (table - high.astype(np.float32)).astype(ml_dtypes.bfloat16)
    return np.concatenate([high, low], axis=0)


def nt_dot(a, b):
    return lax.dot_general(a, b, (((1,), (1,)), ((), ())), preferred_element_type=jnp.float32)


def nn_dot(a, b):
    return lax.dot_general(a, b, (((1,), (0,)), ((), ())), preferred_element_type=jnp.float32)


def pick_body(index_ref, block_ref, raw_ref, out_ref, chan_ref, sel_ref, held_ref, got_ref, sems, out_sems):
    segs, count, _ = raw_ref.shape
    parts = sems.shape[0]
    size = segs // parts
    copies = []
    for i in range(parts):
        at = pl.ds(i * size, size)
        copies.append(pltpu.make_async_copy(raw_ref.at[at], held_ref.at[at], sems.at[i]))
        copies[-1].start()
    first = lax.axis_index("ch") * count
    for s in range(SOURCES):
        rank = jnp.int32(0)
        for t in range(s):
            rank += jnp.where(block_ref[t] == block_ref[s], 1, 0).astype(jnp.int32)
        chan_ref[block_ref[s] * PER_BLOCK + rank] = index_ref[s] - first
    lane = lax.broadcasted_iota(jnp.int32, (8, count), 1)
    sub = lax.broadcasted_iota(jnp.int32, (8, count), 0)
    for q in range(SOURCES):
        hit = jnp.where(lane == chan_ref[q], 1.0, 0.0)
        for g in range(8):
            sel_ref[q * 8 : q * 8 + 8, g * count : (g + 1) * count] = jnp.where(sub == g, hit, 0.0)
    select = sel_ref[...].astype(jnp.bfloat16)
    outs = []
    for h in range(segs // 8):
        total = None
        for i in range(8 * h // size, (8 * h + 8) // size):
            copies[i].wait()
            rows = held_ref[i * size : (i + 1) * size].reshape(size * count, SEGLEN)
            g = (i * size) % 8
            term = nn_dot(select[:, g * count : (g + size) * count], rows)
            total = term if total is None else total + term
        got_ref[h] = total.astype(jnp.bfloat16).reshape(SOURCES, 8, SEGLEN)
        outs.append(pltpu.make_async_copy(got_ref.at[h], out_ref.at[:, h], out_sems.at[h]))
        outs[-1].start()
    for copy in outs:
        copy.wait()


def pick(raw, source_index, source_block):
    segs, count, length = raw.shape
    parts = 8
    return pl.pallas_call(
        pick_body,
        grid_spec=pltpu.PrefetchScalarGridSpec(
            num_scalar_prefetch=2,
            grid=(1,),
            in_specs=[pl.BlockSpec(memory_space=pl.ANY)],
            out_specs=pl.BlockSpec(memory_space=pl.ANY),
            scratch_shapes=[
                pltpu.SMEM((SOURCES,), jnp.int32),
                pltpu.VMEM((SOURCES * 8, 8 * count), jnp.float32),
                pltpu.VMEM(raw.shape, raw.dtype),
                pltpu.VMEM((segs // 8, SOURCES, 8, length), raw.dtype),
                pltpu.SemaphoreType.DMA((parts,)),
                pltpu.SemaphoreType.DMA((segs // 8,)),
            ],
        ),
        out_shape=jax.ShapeDtypeStruct((SOURCES, segs // 8, 8, length), jnp.bfloat16),
        compiler_params=pltpu.CompilerParams(vmem_limit_bytes=PICK_VMEM),
        cost_estimate=pl.CostEstimate(flops=2 * 10**8, bytes_accessed=5 * 10**6, transcendentals=0),
        name="pick",
    )(source_index, source_block, raw)


def source_body(parts_ref, table_ref, after_ref, out_ref):
    total = jnp.sum(parts_ref[...].astype(jnp.float32), axis=0)
    spectrum = nt_dot(total.astype(jnp.bfloat16), table_ref[...])
    real = spectrum[:, :FREQS]
    imag = spectrum[:, FREQS:]
    amplitude = jnp.sqrt(real * real + imag * imag)
    place = lax.broadcasted_iota(jnp.int32, amplitude.shape, 1)
    smoothed = amplitude
    for shift in range(1, SMOOTH + 1):
        later = pltpu.roll(amplitude, FREQS - shift, 1)
        smoothed += jnp.where(place < FREQS - shift, later, 0.0)
        earlier = pltpu.roll(amplitude, shift, 1)
        smoothed += jnp.where(place >= shift, earlier, 0.0)
    level = jnp.sum(amplitude, axis=1, keepdims=True) * (1.0 / FREQS)
    divisor = smoothed / (2 * SMOOTH + 1) + WATER * level + EPS
    real = (real / divisor).astype(jnp.bfloat16).astype(jnp.float32)
    imag = (imag / divisor).astype(jnp.bfloat16).astype(jnp.float32)
    sub = lax.broadcasted_iota(jnp.int32, (8, 128), 0)
    lane = lax.broadcasted_iota(jnp.int32, (8, 128), 1)
    block = (lane // 8) % 8

    def turn(x):
        for s in (4, 2, 1):
            down = pltpu.roll(pltpu.roll(x, s, 0), 128 - 8 * s, 1)
            up = pltpu.roll(pltpu.roll(x, 8 - s, 0), 8 * s, 1)
            low_row = (sub & s) == 0
            low_block = (block & s) == 0
            x = jnp.where(low_row == low_block, x, jnp.where(low_row, up, down))
        return x

    rows = []
    for j in range(FREQS // 128):
        re = turn(real[:, j * 128 : (j + 1) * 128])
        im = turn(imag[:, j * 128 : (j + 1) * 128])
        rows.append(jnp.where(lane < 64, re, pltpu.roll(im, 64, 1)))
        rows.append(jnp.where(lane < 64, pltpu.roll(re, 64, 1), im))
    packed = jnp.concatenate(rows, axis=0).astype(jnp.bfloat16)
    out_ref[...] = jnp.broadcast_to(packed[None], out_ref.shape)


def source_rows(parts, table, after):
    return pl.pallas_call(
        source_body,
        out_shape=jax.ShapeDtypeStruct((parts.shape[0], GROUPS, 128), jnp.bfloat16),
        in_specs=[pl.BlockSpec(memory_space=pltpu.VMEM)] * 2 + [pl.BlockSpec(memory_space=pl.ANY)],
        out_specs=pl.BlockSpec(memory_space=pltpu.VMEM),
        compiler_params=pltpu.CompilerParams(vmem_limit_bytes=SOURCE_VMEM),
        cost_estimate=pl.CostEstimate(flops=2 * 8 * 1024 * 1024, bytes_accessed=3 * 10**6, transcendentals=0),
        name="source_rows",
    )(parts, table, after)


def whiten_body(raw_ref, table_ref, out_ref, done_ref, spec_ref, amp_ref):
    count = raw_ref.shape[1]
    width = 2 * count
    step = 32
    size = step + 16
    zero = jnp.zeros((8, width), jnp.float32)
    done_ref[...] = zero[:, :128]
    amp_ref[0:8, :] = zero
    amp_ref[FREQS + 8 : FREQS + 16, :] = zero
    spec_ref[...] = nt_dot(table_ref[...], raw_ref[...].reshape(width, SEGLEN))
    level = zero
    for f in range(0, FREQS, step):
        real = spec_ref[f : f + step, :]
        imag = spec_ref[FREQS + f : FREQS + f + step, :]
        amplitude = jnp.sqrt(real * real + imag * imag)
        amp_ref[8 + f : 8 + f + step, :] = amplitude
        for i in range(0, step, 8):
            level += amplitude[i : i + 8]
    level = jnp.sum(level, axis=0, keepdims=True) * (WATER / FREQS) + EPS
    for f in range(0, FREQS, step):
        a = amp_ref[f : f + size, :]
        s2 = a + pltpu.roll(a, size - 1, 0)
        s4 = s2 + pltpu.roll(s2, size - 2, 0)
        s9 = s4 + pltpu.roll(s4, 4, 0) + pltpu.roll(a, size - 4, 0)
        inverse = 1.0 / (s9[8 : 8 + step] * (1.0 / (2 * SMOOTH + 1)) + level)
        real = spec_ref[f : f + step, :] * inverse
        imag = spec_ref[FREQS + f : FREQS + f + step, :] * inverse
        for part, value in ((0, real), (1, imag)):
            for i in range(0, step, 8):
                both = jnp.concatenate([value[i : i + 8, :count], value[i : i + 8, count:]], axis=0)
                out_ref[(f + i) // 8, part, 0] = both.astype(jnp.bfloat16)


def whiten(raw, table, half):
    segs, count, length = raw.shape
    pairs = segs // 4
    out, done = pl.pallas_call(
        whiten_body,
        grid=(pairs,),
        in_specs=[
            pl.BlockSpec((2, count, length), lambda i: (i + half * pairs, 0, 0)),
            pl.BlockSpec((2 * FREQS, length), lambda i: (0, 0)),
        ],
        out_specs=[
            pl.BlockSpec((GROUPS, 2, 1, 16, count), lambda i: (0, 0, i, 0, 0)),
            pl.BlockSpec((8, 128), lambda i: (0, 0)),
        ],
        out_shape=[
            jax.ShapeDtypeStruct((GROUPS, 2, pairs, 16, count), jnp.bfloat16),
            jax.ShapeDtypeStruct((8, 128), jnp.float32),
        ],
        scratch_shapes=[
            pltpu.VMEM((2 * FREQS, 2 * count), jnp.float32),
            pltpu.VMEM((FREQS + 16, 2 * count), jnp.float32),
        ],
        compiler_params=pltpu.CompilerParams(vmem_limit_bytes=WHITEN_VMEM),
        cost_estimate=pl.CostEstimate(
            flops=2 * 1024 * 1024 * 1024, bytes_accessed=6 * 10**6, transcendentals=10**6
        ),
        name=f"whiten{half}",
    )(raw, table)
    return out.reshape(GROUPS, 32 * pairs, count), done


def correlate_body(src_ref, w0_ref, w1_ref, lag_ref, *refs):
    out_refs = refs[:4]
    s_ref, w_ref, table_ref, high_ref, low_ref, sum_ref, sems, table_sem = refs[4:]
    count = w0_ref.shape[2]
    deep = w0_ref.shape[1]
    parts = sems.shape[0]
    blocks = GROUPS // parts

    def load(i, half):
        at = pl.ds(i * blocks, blocks)
        source = (w0_ref, w1_ref)[half]
        return pltpu.make_async_copy(
            source.at[at], w_ref.at[at, pl.ds(half * deep, deep)], sems.at[i, half]
        )

    for i in range(parts):
        load(i, 0).start()
        load(i, 1).start()
    table_copy = pltpu.make_async_copy(lag_ref, table_ref, table_sem)
    table_copy.start()

    lanes = lax.broadcasted_iota(jnp.int32, (GROUPS, 128), 1)
    for i in range(2 * SOURCES):
        value = src_ref[i].astype(jnp.float32)
        s_ref[0, i] = value
        turned = pltpu.roll(value, 64, 1)
        s_ref[1, i] = jnp.where(lanes < 64, -turned, turned)

    sub = lax.broadcasted_iota(jnp.int32, (8, 128), 0)
    lane = lax.broadcasted_iota(jnp.int32, (8, 128), 1)
    diagonal = (lane % 8) == sub

    def chunk(i, carry):
        load(i, 0).wait()
        load(i, 1).wait()
        for j in range(blocks):
            b = i * blocks + j
            tiles = []
            for q in range(SOURCES):
                halves = []
                for h in range(2):
                    pieces = []
                    for r in range(2):
                        row = jnp.broadcast_to(s_ref[r, 2 * q + h, pl.ds(b, 1), :], (8, 128))
                        pieces.append(jnp.where(diagonal, row, 0.0))
                    halves.append(jnp.concatenate(pieces, axis=0).astype(jnp.bfloat16))
                tiles.append(jnp.concatenate(halves, axis=1))
            cross = nn_dot(jnp.concatenate(tiles, axis=0), w_ref[b])
            high = cross.astype(jnp.bfloat16)
            low = (cross - high.astype(jnp.float32)).astype(jnp.bfloat16)
            at = pl.ds(pl.multiple_of(b * 16, 16), 16)
            for q in range(SOURCES):
                cols = slice((q % 2) * count, (q % 2 + 1) * count)
                high_ref[q // 2, at, cols] = high[q * 16 : q * 16 + 16]
                low_ref[q // 2, at, cols] = low[q * 16 : q * 16 + 16]
        return carry

    lax.fori_loop(0, parts, chunk, 0)
    table_copy.wait()
    me = lax.axis_index("seg")
    share = count // 4
    for p in range(SOURCES // 2):
        first = nn_dot(table_ref[...], high_ref[p])
        second = nn_dot(table_ref[:LAGS, :], low_ref[p])
        total = first[:LAGS] + (first[LAGS:] + second)
        for i in range(2):
            sum_ref[2 * p + i] = total[:, i * count : (i + 1) * count].T

    def part(r):
        return sum_ref[:, pl.ds(pl.multiple_of((me ^ r) * share, share), share), :]

    for r, out_ref in enumerate(out_refs):
        out_ref[...] = part(r)


def correlate(src, w0, w1, lag):
    count = w0.shape[2]
    parts = 8
    share = count // 4
    shape = (SOURCES, share, LAGS)
    vmem = pl.BlockSpec(memory_space=pltpu.VMEM)
    anywhere = pl.BlockSpec(memory_space=pl.ANY)
    return pl.pallas_call(
        correlate_body,
        in_specs=[vmem, anywhere, anywhere, anywhere],
        out_specs=[vmem] * 4,
        out_shape=[jax.ShapeDtypeStruct(shape, jnp.float32)] * 4,
        scratch_shapes=[
            pltpu.VMEM((2, 2 * SOURCES, GROUPS, 128), jnp.float32),
            pltpu.VMEM((GROUPS, 2 * w0.shape[1], count), jnp.bfloat16),
            pltpu.VMEM(lag.shape, lag.dtype),
            pltpu.VMEM((SOURCES // 2, 2 * FREQS, 2 * count), jnp.bfloat16),
            pltpu.VMEM((SOURCES // 2, 2 * FREQS, 2 * count), jnp.bfloat16),
            pltpu.VMEM((SOURCES, count, LAGS), jnp.float32),
            pltpu.SemaphoreType.DMA((parts, 2)),
            pltpu.SemaphoreType.DMA,
        ],
        compiler_params=pltpu.CompilerParams(vmem_limit_bytes=CORRELATE_VMEM),
        cost_estimate=pl.CostEstimate(flops=3 * 10**9, bytes_accessed=6 * 10**6, transcendentals=0),
        name="correlate",
    )(src, w0, w1, lag)


def chip_sum_body(mine_ref, core_ref, out_ref):
    out_ref[...] = (mine_ref[...] + core_ref[...]).astype(jnp.bfloat16)


def chip_sum(mine, core):
    return pl.pallas_call(
        chip_sum_body,
        in_specs=[pl.BlockSpec(memory_space=pltpu.VMEM)] * 2,
        out_specs=pl.BlockSpec(memory_space=pltpu.VMEM),
        out_shape=jax.ShapeDtypeStruct(mine.shape, jnp.bfloat16),
        compiler_params=pltpu.CompilerParams(vmem_limit_bytes=SUM_VMEM),
        cost_estimate=pl.CostEstimate(flops=10**5, bytes_accessed=10**6, transcendentals=0),
        name="chip_sum",
    )(mine, core)


def gather_sum_body(mine_ref, core_ref, far_ref, out_ref):
    total = (mine_ref[...] + core_ref[...]) + far_ref[...].astype(jnp.float32)
    for q in range(SOURCES):
        out_ref[:, q, :] = total[q]


def gather_sum(mine, core, far):
    shape = mine.shape
    return pl.pallas_call(
        gather_sum_body,
        in_specs=[pl.BlockSpec(memory_space=pltpu.VMEM)] * 3,
        out_specs=pl.BlockSpec(memory_space=pltpu.VMEM),
        out_shape=jax.ShapeDtypeStruct((shape[1], shape[0], shape[2]), jnp.float32),
        compiler_params=pltpu.CompilerParams(vmem_limit_bytes=SUM_VMEM),
        cost_estimate=pl.CostEstimate(flops=10**6, bytes_accessed=10**6, transcendentals=0),
        name="gather_sum",
    )(mine, core, far)


def local(raw, source_index, source_block):
    segs = raw.shape[0] * lax.axis_size("seg")
    ways = lax.axis_size("ch")
    table = jnp.asarray(dft_rows())
    lag = jnp.asarray(lag_rows(1.0 / (FREQS * segs)))
    picked = pick(raw, source_index, source_block)
    parts = lax.all_to_all(picked.reshape(ways, 8, SEGLEN), "ch", 0, 0)
    w0, done = whiten(raw, table, 0)
    spread = source_rows(parts, table, done)
    src = lax.all_to_all(spread, "ch", 0, 0)
    w1, _ = whiten(raw, table, 1)
    parts = correlate(src, w0, w1, lag)

    def swap(x, r):
        return lax.ppermute(x, "seg", [(i, i ^ r) for i in range(4)])

    far = swap(chip_sum(parts[2], swap(parts[3], 1)), 2)
    return gather_sum(parts[0], swap(parts[1], 1), far)


def solution(mesh):
    return jax.shard_map(
        local,
        mesh=mesh,
        in_specs=(P("seg", "ch", None), P(), P()),
        out_specs=P(("ch", "seg"), None, None),
        check_vma=False,
    )
```

```python
import functools

import jax
import jax.numpy as jnp
import ml_dtypes
import numpy as np
from jax import lax
from jax.experimental import pallas as pl
from jax.experimental.pallas import tpu as pltpu
from jax.sharding import PartitionSpec as P

SEGLEN = 1024
FREQS = 512
HALFLAG = 64
LAGS = 128
SMOOTH = 4
SOURCES = 16
PER_BLOCK = 4
WATER = 0.1
EPS = 1e-06

GROUPS = FREQS // 8
ROWS = 16
PICK_VMEM = 58 << 20
WHITEN_VMEM = 52 << 20
SOURCE_VMEM = 48 << 20
CORRELATE_VMEM = 52 << 20
SUM_VMEM = 14 << 20


def dft_rows():
    bins = np.arange(1, FREQS + 1)[:, None]
    times = np.arange(SEGLEN)[None, :]
    phase = ((bins * times) % SEGLEN).astype(np.float32) * np.float32(2.0 * np.pi / SEGLEN)
    table = np.concatenate([np.cos(phase), -np.sin(phase)], axis=0)
    return table.astype(ml_dtypes.bfloat16)


def lag_rows(scale):
    bins = np.arange(1, FREQS + 1)[None, :]
    lags = np.arange(LAGS)[:, None] - HALFLAG
    theta = ((bins * lags) % SEGLEN).astype(np.float32) * np.float32(2.0 * np.pi / SEGLEN)
    cos = np.cos(theta).reshape(LAGS, GROUPS, 1, 8)
    sin = np.sin(theta).reshape(LAGS, GROUPS, 1, 8)
    table = np.concatenate([cos, sin], axis=2).reshape(LAGS, 2 * FREQS) * np.float32(scale)
    high = table.astype(ml_dtypes.bfloat16)
    low = (table - high.astype(np.float32)).astype(ml_dtypes.bfloat16)
    return np.concatenate([high, low], axis=0)


def nt_dot(a, b):
    return lax.dot_general(a, b, (((1,), (1,)), ((), ())), preferred_element_type=jnp.float32)


def nn_dot(a, b):
    return lax.dot_general(a, b, (((1,), (0,)), ((), ())), preferred_element_type=jnp.float32)


def pick_body(index_ref, block_ref, raw_ref, out_ref, chan_ref, held_ref, got_ref, zero_ref, sems, out_sems):
    segs, count, _ = raw_ref.shape
    first = lax.axis_index("ch") * count
    for s in range(SOURCES):
        rank = jnp.int32(0)
        for t in range(s):
            rank += jnp.where(block_ref[t] == block_ref[s], 1, 0).astype(jnp.int32)
        chan_ref[block_ref[s] * PER_BLOCK + rank] = index_ref[s] - first

    def ours(q):
        return (chan_ref[q] >= 0) & (chan_ref[q] < count)

    def load(q):
        start = pl.multiple_of(jnp.clip(chan_ref[q], 0, count - 1) // ROWS * ROWS, ROWS)
        return pltpu.make_async_copy(raw_ref.at[:, pl.ds(start, ROWS)], held_ref.at[q], sems.at[q])

    def store(q, source):
        return pltpu.make_async_copy(source, out_ref.at[q], out_sems.at[q])

    for q in range(SOURCES):
        pl.when(ours(q))(lambda q=q: load(q).start())
    zero_ref[...] = jnp.zeros_like(zero_ref)
    for q in range(SOURCES):
        pl.when(jnp.logical_not(ours(q)))(lambda q=q: store(q, zero_ref).start())
    row = lax.broadcasted_iota(jnp.int32, (segs, segs * ROWS), 0)
    column = lax.broadcasted_iota(jnp.int32, (segs, segs * ROWS), 1)
    for q in range(SOURCES):

        @pl.when(ours(q))
        def _(q=q):
            load(q).wait()
            hit = column == row * ROWS + chan_ref[q] % ROWS
            rows = held_ref[q].reshape(segs * ROWS, SEGLEN)
            got = nn_dot(jnp.where(hit, 1.0, 0.0).astype(jnp.bfloat16), rows)
            got_ref[q] = got.astype(jnp.bfloat16).reshape(segs // 8, 8, SEGLEN)
            store(q, got_ref.at[q]).start()

    for q in range(SOURCES):
        store(q, zero_ref).wait()


def pick(raw, source_index, source_block):
    segs, count, length = raw.shape
    shape = (segs // 8, 8, length)
    return pl.pallas_call(
        pick_body,
        grid_spec=pltpu.PrefetchScalarGridSpec(
            num_scalar_prefetch=2,
            grid=(1,),
            in_specs=[pl.BlockSpec(memory_space=pl.ANY)],
            out_specs=pl.BlockSpec(memory_space=pl.ANY),
            scratch_shapes=[
                pltpu.SMEM((SOURCES,), jnp.int32),
                pltpu.VMEM((SOURCES, segs, ROWS, length), raw.dtype),
                pltpu.VMEM((SOURCES, *shape), raw.dtype),
                pltpu.VMEM(shape, raw.dtype),
                pltpu.SemaphoreType.DMA((SOURCES,)),
                pltpu.SemaphoreType.DMA((SOURCES,)),
            ],
        ),
        out_shape=jax.ShapeDtypeStruct((SOURCES, *shape), jnp.bfloat16),
        compiler_params=pltpu.CompilerParams(vmem_limit_bytes=PICK_VMEM),
        cost_estimate=pl.CostEstimate(flops=10**8, bytes_accessed=3 * 10**6, transcendentals=0),
        name="pick",
    )(source_index, source_block, raw)


def source_body(parts_ref, table_ref, after_ref, out_ref):
    total = jnp.sum(parts_ref[...].astype(jnp.float32), axis=0)
    spectrum = nt_dot(total.astype(jnp.bfloat16), table_ref[...])
    real = spectrum[:, :FREQS]
    imag = spectrum[:, FREQS:]
    amplitude = jnp.sqrt(real * real + imag * imag)
    place = lax.broadcasted_iota(jnp.int32, amplitude.shape, 1)
    smoothed = amplitude
    for shift in range(1, SMOOTH + 1):
        later = pltpu.roll(amplitude, FREQS - shift, 1)
        smoothed += jnp.where(place < FREQS - shift, later, 0.0)
        earlier = pltpu.roll(amplitude, shift, 1)
        smoothed += jnp.where(place >= shift, earlier, 0.0)
    level = jnp.sum(amplitude, axis=1, keepdims=True) * (1.0 / FREQS)
    divisor = smoothed / (2 * SMOOTH + 1) + WATER * level + EPS
    real = (real / divisor).astype(jnp.bfloat16).astype(jnp.float32)
    imag = (imag / divisor).astype(jnp.bfloat16).astype(jnp.float32)
    sub = lax.broadcasted_iota(jnp.int32, (8, 128), 0)
    lane = lax.broadcasted_iota(jnp.int32, (8, 128), 1)
    block = (lane // 8) % 8

    def turn(x):
        for s in (4, 2, 1):
            down = pltpu.roll(pltpu.roll(x, s, 0), 128 - 8 * s, 1)
            up = pltpu.roll(pltpu.roll(x, 8 - s, 0), 8 * s, 1)
            low_row = (sub & s) == 0
            low_block = (block & s) == 0
            x = jnp.where(low_row == low_block, x, jnp.where(low_row, up, down))
        return x

    rows = []
    for j in range(FREQS // 128):
        re = turn(real[:, j * 128 : (j + 1) * 128])
        im = turn(imag[:, j * 128 : (j + 1) * 128])
        rows.append(jnp.where(lane < 64, re, pltpu.roll(im, 64, 1)))
        rows.append(jnp.where(lane < 64, pltpu.roll(re, 64, 1), im))
    packed = jnp.concatenate(rows, axis=0).astype(jnp.bfloat16)
    out_ref[...] = jnp.broadcast_to(packed[None], out_ref.shape)


def source_rows(parts, table, after):
    return pl.pallas_call(
        source_body,
        out_shape=jax.ShapeDtypeStruct((parts.shape[0], GROUPS, 128), jnp.bfloat16),
        in_specs=[pl.BlockSpec(memory_space=pltpu.VMEM)] * 2 + [pl.BlockSpec(memory_space=pl.ANY)],
        out_specs=pl.BlockSpec(memory_space=pltpu.VMEM),
        compiler_params=pltpu.CompilerParams(vmem_limit_bytes=SOURCE_VMEM),
        cost_estimate=pl.CostEstimate(flops=2 * 8 * 1024 * 1024, bytes_accessed=3 * 10**6, transcendentals=0),
        name="source_rows",
    )(parts, table, after)


def whiten_body(raw_ref, table_ref, out_ref, done_ref, spec_ref, amp_ref):
    count = raw_ref.shape[1]
    width = 2 * count
    step = 32
    size = step + 16
    zero = jnp.zeros((8, width), jnp.float32)
    done_ref[...] = zero[:, :128]
    amp_ref[0:8, :] = zero
    amp_ref[FREQS + 8 : FREQS + 16, :] = zero
    spec_ref[...] = nt_dot(table_ref[...], raw_ref[...].reshape(width, SEGLEN))
    level = zero
    for f in range(0, FREQS, step):
        real = spec_ref[f : f + step, :]
        imag = spec_ref[FREQS + f : FREQS + f + step, :]
        amplitude = jnp.sqrt(real * real + imag * imag)
        amp_ref[8 + f : 8 + f + step, :] = amplitude
        for i in range(0, step, 8):
            level += amplitude[i : i + 8]
    level = jnp.sum(level, axis=0, keepdims=True) * (WATER / FREQS) + EPS
    for f in range(0, FREQS, step):
        a = amp_ref[f : f + size, :]
        s2 = a + pltpu.roll(a, size - 1, 0)
        s4 = s2 + pltpu.roll(s2, size - 2, 0)
        s9 = s4 + pltpu.roll(s4, 4, 0) + pltpu.roll(a, size - 4, 0)
        inverse = 1.0 / (s9[8 : 8 + step] * (1.0 / (2 * SMOOTH + 1)) + level)
        real = spec_ref[f : f + step, :] * inverse
        imag = spec_ref[FREQS + f : FREQS + f + step, :] * inverse
        for part, value in ((0, real), (1, imag)):
            for i in range(0, step, 8):
                both = jnp.concatenate([value[i : i + 8, :count], value[i : i + 8, count:]], axis=0)
                out_ref[(f + i) // 8, part, 0] = both.astype(jnp.bfloat16)


def whiten(raw, table, half):
    segs, count, length = raw.shape
    pairs = segs // 4
    out, done = pl.pallas_call(
        whiten_body,
        grid=(pairs,),
        in_specs=[
            pl.BlockSpec((2, count, length), lambda i: (i + half * pairs, 0, 0)),
            pl.BlockSpec((2 * FREQS, length), lambda i: (0, 0)),
        ],
        out_specs=[
            pl.BlockSpec((GROUPS, 2, 1, 16, count), lambda i: (0, 0, i, 0, 0)),
            pl.BlockSpec((8, 128), lambda i: (0, 0)),
        ],
        out_shape=[
            jax.ShapeDtypeStruct((GROUPS, 2, pairs, 16, count), jnp.bfloat16),
            jax.ShapeDtypeStruct((8, 128), jnp.float32),
        ],
        scratch_shapes=[
            pltpu.VMEM((2 * FREQS, 2 * count), jnp.float32),
            pltpu.VMEM((FREQS + 16, 2 * count), jnp.float32),
        ],
        compiler_params=pltpu.CompilerParams(vmem_limit_bytes=WHITEN_VMEM),
        cost_estimate=pl.CostEstimate(
            flops=2 * 1024 * 1024 * 1024, bytes_accessed=6 * 10**6, transcendentals=10**6
        ),
        name=f"whiten{half}",
    )(raw, table)
    return out.reshape(GROUPS, 32 * pairs, count), done


def correlate_body(src_ref, w0_ref, w1_ref, lag_ref, *refs):
    out_refs = refs[:4]
    s_ref, w_ref, table_ref, high_ref, low_ref, sum_ref, sems, table_sem = refs[4:]
    count = w0_ref.shape[2]
    deep = w0_ref.shape[1]
    parts = sems.shape[0]
    blocks = GROUPS // parts

    def load(i, half):
        at = pl.ds(i * blocks, blocks)
        source = (w0_ref, w1_ref)[half]
        return pltpu.make_async_copy(
            source.at[at], w_ref.at[at, pl.ds(half * deep, deep)], sems.at[i, half]
        )

    for i in range(parts):
        load(i, 0).start()
        load(i, 1).start()
    table_copy = pltpu.make_async_copy(lag_ref, table_ref, table_sem)
    table_copy.start()

    lanes = lax.broadcasted_iota(jnp.int32, (GROUPS, 128), 1)
    for i in range(2 * SOURCES):
        value = src_ref[i].astype(jnp.float32)
        s_ref[0, i] = value
        turned = pltpu.roll(value, 64, 1)
        s_ref[1, i] = jnp.where(lanes < 64, -turned, turned)

    sub = lax.broadcasted_iota(jnp.int32, (8, 128), 0)
    lane = lax.broadcasted_iota(jnp.int32, (8, 128), 1)
    diagonal = (lane % 8) == sub

    def chunk(i):
        load(i, 0).wait()
        load(i, 1).wait()
        for j in range(blocks):
            b = i * blocks + j
            tiles = []
            for q in range(SOURCES):
                halves = []
                for h in range(2):
                    pieces = []
                    for r in range(2):
                        row = jnp.broadcast_to(s_ref[r, 2 * q + h, b : b + 1, :], (8, 128))
                        pieces.append(jnp.where(diagonal, row, 0.0))
                    halves.append(jnp.concatenate(pieces, axis=0).astype(jnp.bfloat16))
                tiles.append(jnp.concatenate(halves, axis=1))
            cross = nn_dot(jnp.concatenate(tiles, axis=0), w_ref[b])
            high = cross.astype(jnp.bfloat16)
            low = (cross - high.astype(jnp.float32)).astype(jnp.bfloat16)
            at = slice(b * 16, b * 16 + 16)
            for q in range(SOURCES):
                cols = slice((q % 2) * count, (q % 2 + 1) * count)
                high_ref[q // 2, at, cols] = high[q * 16 : q * 16 + 16]
                low_ref[q // 2, at, cols] = low[q * 16 : q * 16 + 16]

    for i in range(parts):
        chunk(i)
    table_copy.wait()
    me = lax.axis_index("seg")
    share = count // 4
    for p in range(SOURCES // 2):
        first = nn_dot(table_ref[...], high_ref[p])
        second = nn_dot(table_ref[:LAGS, :], low_ref[p])
        total = first[:LAGS] + (first[LAGS:] + second)
        for i in range(2):
            sum_ref[2 * p + i] = total[:, i * count : (i + 1) * count].T

    def part(r):
        return sum_ref[:, pl.ds(pl.multiple_of((me ^ r) * share, share), share), :]

    for r, out_ref in enumerate(out_refs):
        out_ref[...] = part(r)


def correlate(src, w0, w1, lag):
    count = w0.shape[2]
    parts = 8
    share = count // 4
    shape = (SOURCES, share, LAGS)
    vmem = pl.BlockSpec(memory_space=pltpu.VMEM)
    anywhere = pl.BlockSpec(memory_space=pl.ANY)
    return pl.pallas_call(
        correlate_body,
        in_specs=[vmem, anywhere, anywhere, anywhere],
        out_specs=[vmem] * 4,
        out_shape=[jax.ShapeDtypeStruct(shape, jnp.float32)] * 4,
        scratch_shapes=[
            pltpu.VMEM((2, 2 * SOURCES, GROUPS, 128), jnp.float32),
            pltpu.VMEM((GROUPS, 2 * w0.shape[1], count), jnp.bfloat16),
            pltpu.VMEM(lag.shape, lag.dtype),
            pltpu.VMEM((SOURCES // 2, 2 * FREQS, 2 * count), jnp.bfloat16),
            pltpu.VMEM((SOURCES // 2, 2 * FREQS, 2 * count), jnp.bfloat16),
            pltpu.VMEM((SOURCES, count, LAGS), jnp.float32),
            pltpu.SemaphoreType.DMA((parts, 2)),
            pltpu.SemaphoreType.DMA,
        ],
        compiler_params=pltpu.CompilerParams(vmem_limit_bytes=CORRELATE_VMEM),
        cost_estimate=pl.CostEstimate(flops=3 * 10**9, bytes_accessed=6 * 10**6, transcendentals=0),
        name="correlate",
    )(src, w0, w1, lag)


def chip_sum_body(mine_ref, core_ref, out_ref):
    out_ref[...] = (mine_ref[...] + core_ref[...]).astype(jnp.bfloat16)


def chip_sum(mine, core):
    return pl.pallas_call(
        chip_sum_body,
        in_specs=[pl.BlockSpec(memory_space=pltpu.VMEM)] * 2,
        out_specs=pl.BlockSpec(memory_space=pltpu.VMEM),
        out_shape=jax.ShapeDtypeStruct(mine.shape, jnp.bfloat16),
        compiler_params=pltpu.CompilerParams(vmem_limit_bytes=SUM_VMEM),
        cost_estimate=pl.CostEstimate(flops=10**5, bytes_accessed=10**6, transcendentals=0),
        name="chip_sum",
    )(mine, core)


def gather_sum_body(mine_ref, core_ref, far_ref, out_ref):
    total = (mine_ref[...] + core_ref[...]) + far_ref[...].astype(jnp.float32)
    for q in range(SOURCES):
        out_ref[:, q, :] = total[q]


def gather_sum(mine, core, far):
    shape = mine.shape
    return pl.pallas_call(
        gather_sum_body,
        in_specs=[pl.BlockSpec(memory_space=pltpu.VMEM)] * 3,
        out_specs=pl.BlockSpec(memory_space=pltpu.VMEM),
        out_shape=jax.ShapeDtypeStruct((shape[1], shape[0], shape[2]), jnp.float32),
        compiler_params=pltpu.CompilerParams(vmem_limit_bytes=SUM_VMEM),
        cost_estimate=pl.CostEstimate(flops=10**6, bytes_accessed=10**6, transcendentals=0),
        name="gather_sum",
    )(mine, core, far)


def local(raw, source_index, source_block):
    segs = raw.shape[0] * lax.axis_size("seg")
    ways = lax.axis_size("ch")
    table = jnp.asarray(dft_rows())
    lag = jnp.asarray(lag_rows(1.0 / (FREQS * segs)))
    picked = pick(raw, source_index, source_block)
    parts = lax.all_to_all(picked.reshape(ways, 8, SEGLEN), "ch", 0, 0)
    w0, done = whiten(raw, table, 0)
    spread = source_rows(parts, table, done)
    src = lax.all_to_all(spread, "ch", 0, 0)
    w1, _ = whiten(raw, table, 1)
    parts = correlate(src, w0, w1, lag)

    def swap(x, r):
        return lax.ppermute(x, "seg", [(i, i ^ r) for i in range(4)])

    far = swap(chip_sum(parts[2], swap(parts[3], 1)), 2)
    return gather_sum(parts[0], swap(parts[1], 1), far)


def solution(mesh):
    return jax.shard_map(
        local,
        mesh=mesh,
        in_specs=(P("seg", "ch", None), P(), P()),
        out_specs=P(("ch", "seg"), None, None),
        check_vma=False,
    )
```

```python
import functools

import jax
import jax.numpy as jnp
import ml_dtypes
import numpy as np
from jax import lax
from jax.experimental import pallas as pl
from jax.experimental.pallas import tpu as pltpu
from jax.sharding import PartitionSpec as P

SEGLEN = 1024
FREQS = 512
HALFLAG = 64
LAGS = 128
SMOOTH = 4
SOURCES = 16
PER_BLOCK = 4
WATER = 0.1
EPS = 1e-06

GROUPS = FREQS // 8
ROWS = 16
PARTS = (0, 8, 32, 64)
PICK_VMEM = 58 << 20
WHITEN_VMEM = 52 << 20
SOURCE_VMEM = 48 << 20
CORRELATE_VMEM = 52 << 20
SUM_VMEM = 14 << 20


def dft_rows():
    bins = np.arange(1, FREQS + 1)[:, None]
    times = np.arange(SEGLEN)[None, :]
    phase = ((bins * times) % SEGLEN).astype(np.float32) * np.float32(2.0 * np.pi / SEGLEN)
    table = np.concatenate([np.cos(phase), -np.sin(phase)], axis=0)
    return table.astype(ml_dtypes.bfloat16)


def lag_rows(scale):
    bins = np.arange(1, FREQS + 1)[None, :]
    lags = np.arange(LAGS)[:, None] - HALFLAG
    theta = ((bins * lags) % SEGLEN).astype(np.float32) * np.float32(2.0 * np.pi / SEGLEN)
    cos = np.cos(theta).reshape(LAGS, GROUPS, 1, 8)
    sin = np.sin(theta).reshape(LAGS, GROUPS, 1, 8)
    table = np.concatenate([cos, sin], axis=2).reshape(LAGS, 2 * FREQS) * np.float32(scale)
    high = table.astype(ml_dtypes.bfloat16)
    low = (table - high.astype(np.float32)).astype(ml_dtypes.bfloat16)
    return np.concatenate([high, low], axis=0)


def nt_dot(a, b):
    return lax.dot_general(a, b, (((1,), (1,)), ((), ())), preferred_element_type=jnp.float32)


def nn_dot(a, b):
    return lax.dot_general(a, b, (((1,), (0,)), ((), ())), preferred_element_type=jnp.float32)


def pick_body(index_ref, block_ref, raw_ref, out_ref, chan_ref, held_ref, got_ref, zero_ref, sems, out_sems):
    segs, count, _ = raw_ref.shape
    first = lax.axis_index("ch") * count
    for s in range(SOURCES):
        rank = jnp.int32(0)
        for t in range(s):
            rank += jnp.where(block_ref[t] == block_ref[s], 1, 0).astype(jnp.int32)
        chan_ref[block_ref[s] * PER_BLOCK + rank] = index_ref[s] - first

    def ours(q):
        return (chan_ref[q] >= 0) & (chan_ref[q] < count)

    def load(q):
        start = pl.multiple_of(jnp.clip(chan_ref[q], 0, count - 1) // ROWS * ROWS, ROWS)
        return pltpu.make_async_copy(raw_ref.at[:, pl.ds(start, ROWS)], held_ref.at[q], sems.at[q])

    def store(q, source):
        return pltpu.make_async_copy(source, out_ref.at[q], out_sems.at[q])

    for q in range(SOURCES):
        pl.when(ours(q))(lambda q=q: load(q).start())
    zero_ref[...] = jnp.zeros_like(zero_ref)
    for q in range(SOURCES):
        pl.when(jnp.logical_not(ours(q)))(lambda q=q: store(q, zero_ref).start())
    row = lax.broadcasted_iota(jnp.int32, (segs, segs * ROWS), 0)
    column = lax.broadcasted_iota(jnp.int32, (segs, segs * ROWS), 1)
    for q in range(SOURCES):

        @pl.when(ours(q))
        def _(q=q):
            load(q).wait()
            hit = column == row * ROWS + chan_ref[q] % ROWS
            rows = held_ref[q].reshape(segs * ROWS, SEGLEN)
            got = nn_dot(jnp.where(hit, 1.0, 0.0).astype(jnp.bfloat16), rows)
            got_ref[q] = got.astype(jnp.bfloat16).reshape(segs // 8, 8, SEGLEN)
            store(q, got_ref.at[q]).start()

    for q in range(SOURCES):
        store(q, zero_ref).wait()


def pick(raw, source_index, source_block):
    segs, count, length = raw.shape
    shape = (segs // 8, 8, length)
    return pl.pallas_call(
        pick_body,
        grid_spec=pltpu.PrefetchScalarGridSpec(
            num_scalar_prefetch=2,
            grid=(1,),
            in_specs=[pl.BlockSpec(memory_space=pl.ANY)],
            out_specs=pl.BlockSpec(memory_space=pl.ANY),
            scratch_shapes=[
                pltpu.SMEM((SOURCES,), jnp.int32),
                pltpu.VMEM((SOURCES, segs, ROWS, length), raw.dtype),
                pltpu.VMEM((SOURCES, *shape), raw.dtype),
                pltpu.VMEM(shape, raw.dtype),
                pltpu.SemaphoreType.DMA((SOURCES,)),
                pltpu.SemaphoreType.DMA((SOURCES,)),
            ],
        ),
        out_shape=jax.ShapeDtypeStruct((SOURCES, *shape), jnp.bfloat16),
        compiler_params=pltpu.CompilerParams(vmem_limit_bytes=PICK_VMEM),
        cost_estimate=pl.CostEstimate(flops=10**8, bytes_accessed=3 * 10**6, transcendentals=0),
        name="pick",
    )(source_index, source_block, raw)


def source_body(parts_ref, table_ref, after_ref, out_ref):
    total = jnp.sum(parts_ref[...].astype(jnp.float32), axis=0)
    spectrum = nt_dot(total.astype(jnp.bfloat16), table_ref[...])
    real = spectrum[:, :FREQS]
    imag = spectrum[:, FREQS:]
    amplitude = jnp.sqrt(real * real + imag * imag)
    place = lax.broadcasted_iota(jnp.int32, amplitude.shape, 1)
    smoothed = amplitude
    for shift in range(1, SMOOTH + 1):
        later = pltpu.roll(amplitude, FREQS - shift, 1)
        smoothed += jnp.where(place < FREQS - shift, later, 0.0)
        earlier = pltpu.roll(amplitude, shift, 1)
        smoothed += jnp.where(place >= shift, earlier, 0.0)
    level = jnp.sum(amplitude, axis=1, keepdims=True) * (1.0 / FREQS)
    divisor = smoothed / (2 * SMOOTH + 1) + WATER * level + EPS
    real = (real / divisor).astype(jnp.bfloat16).astype(jnp.float32)
    imag = (imag / divisor).astype(jnp.bfloat16).astype(jnp.float32)
    sub = lax.broadcasted_iota(jnp.int32, (8, 128), 0)
    lane = lax.broadcasted_iota(jnp.int32, (8, 128), 1)
    block = (lane // 8) % 8

    def turn(x):
        for s in (4, 2, 1):
            down = pltpu.roll(pltpu.roll(x, s, 0), 128 - 8 * s, 1)
            up = pltpu.roll(pltpu.roll(x, 8 - s, 0), 8 * s, 1)
            low_row = (sub & s) == 0
            low_block = (block & s) == 0
            x = jnp.where(low_row == low_block, x, jnp.where(low_row, up, down))
        return x

    rows = []
    for j in range(FREQS // 128):
        re = turn(real[:, j * 128 : (j + 1) * 128])
        im = turn(imag[:, j * 128 : (j + 1) * 128])
        rows.append(jnp.where(lane < 64, re, pltpu.roll(im, 64, 1)))
        rows.append(jnp.where(lane < 64, pltpu.roll(re, 64, 1), im))
    packed = jnp.concatenate(rows, axis=0).astype(jnp.bfloat16)
    out_ref[...] = jnp.broadcast_to(packed[None], out_ref.shape)


def source_rows(parts, table, after):
    return pl.pallas_call(
        source_body,
        out_shape=jax.ShapeDtypeStruct((parts.shape[0], GROUPS, 128), jnp.bfloat16),
        in_specs=[pl.BlockSpec(memory_space=pltpu.VMEM)] * 2 + [pl.BlockSpec(memory_space=pl.ANY)],
        out_specs=pl.BlockSpec(memory_space=pltpu.VMEM),
        compiler_params=pltpu.CompilerParams(vmem_limit_bytes=SOURCE_VMEM),
        cost_estimate=pl.CostEstimate(flops=2 * 8 * 1024 * 1024, bytes_accessed=3 * 10**6, transcendentals=0),
        name="source_rows",
    )(parts, table, after)


def whiten_body(raw_ref, half_ref, out_ref, done_ref, spec_ref, amp_ref, table_ref):
    @pl.when(pl.program_id(0) == 0)
    def _():
        row = lax.broadcasted_iota(jnp.int32, half_ref.shape, 0)
        part = half_ref[...]
        table_ref[:, : SEGLEN // 2] = part
        table_ref[:, SEGLEN // 2 :] = jnp.where(row % 2 == 0, -part, part)

    count = raw_ref.shape[1]
    width = 2 * count
    step = 32
    size = step + 16
    zero = jnp.zeros((8, width), jnp.float32)
    amp_ref[0:8, :] = zero
    amp_ref[FREQS + 8 : FREQS + 16, :] = zero
    spec_ref[...] = nt_dot(table_ref[...], raw_ref[...].reshape(width, SEGLEN))
    level = zero
    for f in range(0, FREQS, step):
        real = spec_ref[f : f + step, :]
        imag = spec_ref[FREQS + f : FREQS + f + step, :]
        amplitude = jnp.sqrt(real * real + imag * imag)
        amp_ref[8 + f : 8 + f + step, :] = amplitude
        for i in range(0, step, 8):
            level += amplitude[i : i + 8]
    level = jnp.sum(level, axis=0, keepdims=True) * (WATER / FREQS) + EPS
    for f in range(0, FREQS, step):
        a = amp_ref[f : f + size, :]
        s2 = a + pltpu.roll(a, size - 1, 0)
        s4 = s2 + pltpu.roll(s2, size - 2, 0)
        s9 = s4 + pltpu.roll(s4, 4, 0) + pltpu.roll(a, size - 4, 0)
        inverse = 1.0 / (s9[8 : 8 + step] * (1.0 / (2 * SMOOTH + 1)) + level)
        real = spec_ref[f : f + step, :] * inverse
        imag = spec_ref[FREQS + f : FREQS + f + step, :] * inverse
        for part, value in ((0, real), (1, imag)):
            for i in range(0, step, 8):
                both = jnp.concatenate([value[i : i + 8, :count], value[i : i + 8, count:]], axis=0)
                out_ref[(f + i) // 8, part, 0] = both.astype(jnp.bfloat16)


def whiten(raw, table, half):
    segs, count, length = raw.shape
    pairs = segs // 4
    out, done = pl.pallas_call(
        whiten_body,
        grid=(pairs,),
        in_specs=[
            pl.BlockSpec((2, count, length), lambda i: (i + half * pairs, 0, 0)),
            pl.BlockSpec((2 * FREQS, length // 2), lambda i: (0, 0)),
        ],
        out_specs=[
            pl.BlockSpec((GROUPS, 2, 1, 16, count), lambda i: (0, 0, i, 0, 0)),
            pl.BlockSpec(memory_space=pl.ANY),
        ],
        out_shape=[
            jax.ShapeDtypeStruct((GROUPS, 2, pairs, 16, count), jnp.bfloat16),
            jax.ShapeDtypeStruct((8, 128), jnp.float32),
        ],
        scratch_shapes=[
            pltpu.VMEM((2 * FREQS, 2 * count), jnp.float32),
            pltpu.VMEM((FREQS + 16, 2 * count), jnp.float32),
            pltpu.VMEM((2 * FREQS, length), jnp.bfloat16),
        ],
        compiler_params=pltpu.CompilerParams(vmem_limit_bytes=WHITEN_VMEM),
        cost_estimate=pl.CostEstimate(
            flops=2 * 1024 * 1024 * 1024, bytes_accessed=6 * 10**6, transcendentals=10**6
        ),
        name=f"whiten{half}",
    )(raw, table)
    return out.reshape(GROUPS, 32 * pairs, count), done


def correlate_body(src_ref, w0_ref, w1_ref, lag_ref, *refs):
    out_refs = refs[:4]
    s_ref, w_ref, table_ref, high_ref, low_ref, sum_ref, sems, table_sem = refs[4:]
    count = w0_ref.shape[2]
    deep = w0_ref.shape[1]
    parts = len(PARTS) - 1

    def load(i, half):
        at = pl.ds(PARTS[i], PARTS[i + 1] - PARTS[i])
        source = (w0_ref, w1_ref)[half]
        return pltpu.make_async_copy(
            source.at[at], w_ref.at[at, pl.ds(half * deep, deep)], sems.at[i, half]
        )

    for i in range(parts):
        load(i, 0).start()
        load(i, 1).start()
    table_copy = pltpu.make_async_copy(lag_ref, table_ref, table_sem)
    table_copy.start()

    lanes = lax.broadcasted_iota(jnp.int32, (GROUPS, 128), 1)
    for i in range(2 * SOURCES):
        value = src_ref[i].astype(jnp.float32)
        s_ref[0, i] = value
        turned = pltpu.roll(value, 64, 1)
        s_ref[1, i] = jnp.where(lanes < 64, -turned, turned)

    sub = lax.broadcasted_iota(jnp.int32, (8, 128), 0)
    lane = lax.broadcasted_iota(jnp.int32, (8, 128), 1)
    diagonal = (lane % 8) == sub

    def chunk(i):
        load(i, 0).wait()
        load(i, 1).wait()
        for b in range(PARTS[i], PARTS[i + 1]):
            tiles = []
            for q in range(SOURCES):
                halves = []
                for h in range(2):
                    pieces = []
                    for r in range(2):
                        row = jnp.broadcast_to(s_ref[r, 2 * q + h, b : b + 1, :], (8, 128))
                        pieces.append(jnp.where(diagonal, row, 0.0))
                    halves.append(jnp.concatenate(pieces, axis=0).astype(jnp.bfloat16))
                tiles.append(jnp.concatenate(halves, axis=1))
            cross = nn_dot(jnp.concatenate(tiles, axis=0), w_ref[b])
            high = cross.astype(jnp.bfloat16)
            low = (cross - high.astype(jnp.float32)).astype(jnp.bfloat16)
            at = slice(b * 16, b * 16 + 16)
            for q in range(SOURCES):
                cols = slice((q % 2) * count, (q % 2 + 1) * count)
                high_ref[q // 2, at, cols] = high[q * 16 : q * 16 + 16]
                low_ref[q // 2, at, cols] = low[q * 16 : q * 16 + 16]

    for i in range(parts):
        chunk(i)
    table_copy.wait()
    me = lax.axis_index("seg")
    share = count // 4
    for p in range(SOURCES // 2):
        first = nn_dot(table_ref[...], high_ref[p])
        second = nn_dot(table_ref[:LAGS, :], low_ref[p])
        total = first[:LAGS] + (first[LAGS:] + second)
        for i in range(2):
            sum_ref[2 * p + i] = total[:, i * count : (i + 1) * count].T

    def part(r):
        return sum_ref[:, pl.ds(pl.multiple_of((me ^ r) * share, share), share), :]

    for r, out_ref in enumerate(out_refs):
        out_ref[...] = part(r)


def correlate(src, w0, w1, lag):
    count = w0.shape[2]
    parts = len(PARTS) - 1
    share = count // 4
    shape = (SOURCES, share, LAGS)
    vmem = pl.BlockSpec(memory_space=pltpu.VMEM)
    anywhere = pl.BlockSpec(memory_space=pl.ANY)
    return pl.pallas_call(
        correlate_body,
        in_specs=[vmem, anywhere, anywhere, anywhere],
        out_specs=[vmem] * 4,
        out_shape=[jax.ShapeDtypeStruct(shape, jnp.float32)] * 4,
        scratch_shapes=[
            pltpu.VMEM((2, 2 * SOURCES, GROUPS, 128), jnp.float32),
            pltpu.VMEM((GROUPS, 2 * w0.shape[1], count), jnp.bfloat16),
            pltpu.VMEM(lag.shape, lag.dtype),
            pltpu.VMEM((SOURCES // 2, 2 * FREQS, 2 * count), jnp.bfloat16),
            pltpu.VMEM((SOURCES // 2, 2 * FREQS, 2 * count), jnp.bfloat16),
            pltpu.VMEM((SOURCES, count, LAGS), jnp.float32),
            pltpu.SemaphoreType.DMA((parts, 2)),
            pltpu.SemaphoreType.DMA,
        ],
        compiler_params=pltpu.CompilerParams(vmem_limit_bytes=CORRELATE_VMEM),
        cost_estimate=pl.CostEstimate(flops=3 * 10**9, bytes_accessed=6 * 10**6, transcendentals=0),
        name="correlate",
    )(src, w0, w1, lag)


def chip_sum_body(mine_ref, core_ref, out_ref):
    out_ref[...] = (mine_ref[...] + core_ref[...]).astype(jnp.bfloat16)


def chip_sum(mine, core):
    return pl.pallas_call(
        chip_sum_body,
        in_specs=[pl.BlockSpec(memory_space=pltpu.VMEM)] * 2,
        out_specs=pl.BlockSpec(memory_space=pltpu.VMEM),
        out_shape=jax.ShapeDtypeStruct(mine.shape, jnp.bfloat16),
        compiler_params=pltpu.CompilerParams(vmem_limit_bytes=SUM_VMEM),
        cost_estimate=pl.CostEstimate(flops=10**5, bytes_accessed=10**6, transcendentals=0),
        name="chip_sum",
    )(mine, core)


def gather_sum_body(mine_ref, core_ref, far_ref, out_ref):
    total = (mine_ref[...] + core_ref[...]) + far_ref[...].astype(jnp.float32)
    for q in range(SOURCES):
        out_ref[:, q, :] = total[q]


def gather_sum(mine, core, far):
    shape = mine.shape
    return pl.pallas_call(
        gather_sum_body,
        in_specs=[pl.BlockSpec(memory_space=pltpu.VMEM)] * 3,
        out_specs=pl.BlockSpec(memory_space=pltpu.VMEM),
        out_shape=jax.ShapeDtypeStruct((shape[1], shape[0], shape[2]), jnp.float32),
        compiler_params=pltpu.CompilerParams(vmem_limit_bytes=SUM_VMEM),
        cost_estimate=pl.CostEstimate(flops=10**6, bytes_accessed=10**6, transcendentals=0),
        name="gather_sum",
    )(mine, core, far)


def local(raw, source_index, source_block):
    segs = raw.shape[0] * lax.axis_size("seg")
    ways = lax.axis_size("ch")
    table = jnp.asarray(dft_rows())
    lag = jnp.asarray(lag_rows(1.0 / (FREQS * segs)))
    picked = pick(raw, source_index, source_block)
    parts = lax.all_to_all(picked.reshape(ways, 8, SEGLEN), "ch", 0, 0)
    w0, done = whiten(raw, table, 0)
    spread = source_rows(parts, table, done)
    src = lax.all_to_all(spread, "ch", 0, 0)
    w1, _ = whiten(raw, table, 1)
    parts = correlate(src, w0, w1, lag)

    def swap(x, r):
        return lax.ppermute(x, "seg", [(i, i ^ r) for i in range(4)])

    far = swap(chip_sum(parts[2], swap(parts[3], 1)), 2)
    return gather_sum(parts[0], swap(parts[1], 1), far)


def solution(mesh):
    return jax.shard_map(
        local,
        mesh=mesh,
        in_specs=(P("seg", "ch", None), P(), P()),
        out_specs=P(("ch", "seg"), None, None),
        check_vma=False,
    )
```

```python
import functools

import jax
import jax.numpy as jnp
import ml_dtypes
import numpy as np
from jax import lax
from jax.experimental import pallas as pl
from jax.experimental.pallas import tpu as pltpu
from jax.sharding import PartitionSpec as P

SEGLEN = 1024
FREQS = 512
HALFLAG = 64
LAGS = 128
SMOOTH = 4
SOURCES = 16
PER_BLOCK = 4
WATER = 0.1
EPS = 1e-06

GROUPS = FREQS // 8
ROWS = 16
LAG_ROWS = 80
PARTS = (0, 8, 32, 64)
PICK_VMEM = 58 << 20
WHITEN_VMEM = 52 << 20
SOURCE_VMEM = 48 << 20
CORRELATE_VMEM = 52 << 20
SUM_VMEM = 14 << 20


def dft_rows():
    bins = np.arange(1, FREQS + 1)[:, None]
    times = np.arange(SEGLEN)[None, :]
    phase = ((bins * times) % SEGLEN).astype(np.float32) * np.float32(2.0 * np.pi / SEGLEN)
    table = np.concatenate([np.cos(phase), -np.sin(phase)], axis=0)
    return table.astype(ml_dtypes.bfloat16)


def lag_rows(scale):
    bins = np.arange(1, FREQS + 1)[None, :]
    lags = np.arange(LAG_ROWS)[:, None]
    theta = ((bins * lags) % SEGLEN).astype(np.float32) * np.float32(2.0 * np.pi / SEGLEN)
    table = np.stack([np.cos(theta), np.sin(theta)]) * np.float32(scale)
    table = np.where(lags[None] <= HALFLAG, table, np.float32(0.0)).astype(np.float32)
    high = table.astype(ml_dtypes.bfloat16)
    low = (table - high.astype(np.float32)).astype(ml_dtypes.bfloat16)
    return np.concatenate([high, low], axis=1)


def nt_dot(a, b):
    return lax.dot_general(a, b, (((1,), (1,)), ((), ())), preferred_element_type=jnp.float32)


def nn_dot(a, b):
    return lax.dot_general(a, b, (((1,), (0,)), ((), ())), preferred_element_type=jnp.float32)


def pick_body(index_ref, block_ref, raw_ref, out_ref, chan_ref, held_ref, got_ref, zero_ref, sems, out_sems):
    segs, count, _ = raw_ref.shape
    first = lax.axis_index("ch") * count
    for s in range(SOURCES):
        rank = jnp.int32(0)
        for t in range(s):
            rank += jnp.where(block_ref[t] == block_ref[s], 1, 0).astype(jnp.int32)
        chan_ref[block_ref[s] * PER_BLOCK + rank] = index_ref[s] - first

    def ours(q):
        return (chan_ref[q] >= 0) & (chan_ref[q] < count)

    def load(q):
        start = pl.multiple_of(jnp.clip(chan_ref[q], 0, count - 1) // ROWS * ROWS, ROWS)
        return pltpu.make_async_copy(raw_ref.at[:, pl.ds(start, ROWS)], held_ref.at[q], sems.at[q])

    def store(q, source):
        return pltpu.make_async_copy(source, out_ref.at[q], out_sems.at[q])

    for q in range(SOURCES):
        pl.when(ours(q))(lambda q=q: load(q).start())
    zero_ref[...] = jnp.zeros_like(zero_ref)
    for q in range(SOURCES):
        pl.when(jnp.logical_not(ours(q)))(lambda q=q: store(q, zero_ref).start())
    row = lax.broadcasted_iota(jnp.int32, (segs, segs * ROWS), 0)
    column = lax.broadcasted_iota(jnp.int32, (segs, segs * ROWS), 1)
    for q in range(SOURCES):

        @pl.when(ours(q))
        def _(q=q):
            load(q).wait()
            hit = column == row * ROWS + chan_ref[q] % ROWS
            rows = held_ref[q].reshape(segs * ROWS, SEGLEN)
            got = nn_dot(jnp.where(hit, 1.0, 0.0).astype(jnp.bfloat16), rows)
            got_ref[q] = got.astype(jnp.bfloat16).reshape(segs // 8, 8, SEGLEN)
            store(q, got_ref.at[q]).start()

    for q in range(SOURCES):
        store(q, zero_ref).wait()


def pick(raw, source_index, source_block):
    segs, count, length = raw.shape
    shape = (segs // 8, 8, length)
    return pl.pallas_call(
        pick_body,
        grid_spec=pltpu.PrefetchScalarGridSpec(
            num_scalar_prefetch=2,
            grid=(1,),
            in_specs=[pl.BlockSpec(memory_space=pl.ANY)],
            out_specs=pl.BlockSpec(memory_space=pl.ANY),
            scratch_shapes=[
                pltpu.SMEM((SOURCES,), jnp.int32),
                pltpu.VMEM((SOURCES, segs, ROWS, length), raw.dtype),
                pltpu.VMEM((SOURCES, *shape), raw.dtype),
                pltpu.VMEM(shape, raw.dtype),
                pltpu.SemaphoreType.DMA((SOURCES,)),
                pltpu.SemaphoreType.DMA((SOURCES,)),
            ],
        ),
        out_shape=jax.ShapeDtypeStruct((SOURCES, *shape), jnp.bfloat16),
        compiler_params=pltpu.CompilerParams(vmem_limit_bytes=PICK_VMEM),
        cost_estimate=pl.CostEstimate(flops=10**8, bytes_accessed=3 * 10**6, transcendentals=0),
        name="pick",
    )(source_index, source_block, raw)


def source_body(parts_ref, table_ref, after_ref, out_ref):
    total = jnp.sum(parts_ref[...].astype(jnp.float32), axis=0)
    spectrum = nt_dot(total.astype(jnp.bfloat16), table_ref[...])
    real = spectrum[:, :FREQS]
    imag = spectrum[:, FREQS:]
    amplitude = jnp.sqrt(real * real + imag * imag)
    place = lax.broadcasted_iota(jnp.int32, amplitude.shape, 1)
    smoothed = amplitude
    for shift in range(1, SMOOTH + 1):
        later = pltpu.roll(amplitude, FREQS - shift, 1)
        smoothed += jnp.where(place < FREQS - shift, later, 0.0)
        earlier = pltpu.roll(amplitude, shift, 1)
        smoothed += jnp.where(place >= shift, earlier, 0.0)
    level = jnp.sum(amplitude, axis=1, keepdims=True) * (1.0 / FREQS)
    divisor = smoothed / (2 * SMOOTH + 1) + WATER * level + EPS
    real = (real / divisor).astype(jnp.bfloat16).astype(jnp.float32)
    imag = (imag / divisor).astype(jnp.bfloat16).astype(jnp.float32)
    sub = lax.broadcasted_iota(jnp.int32, (8, 128), 0)
    lane = lax.broadcasted_iota(jnp.int32, (8, 128), 1)
    block = (lane // 8) % 8

    def turn(x):
        for s in (4, 2, 1):
            down = pltpu.roll(pltpu.roll(x, s, 0), 128 - 8 * s, 1)
            up = pltpu.roll(pltpu.roll(x, 8 - s, 0), 8 * s, 1)
            low_row = (sub & s) == 0
            low_block = (block & s) == 0
            x = jnp.where(low_row == low_block, x, jnp.where(low_row, up, down))
        return x

    rows = []
    for j in range(FREQS // 128):
        re = turn(real[:, j * 128 : (j + 1) * 128])
        im = turn(imag[:, j * 128 : (j + 1) * 128])
        rows.append(jnp.where(lane < 64, re, pltpu.roll(im, 64, 1)))
        rows.append(jnp.where(lane < 64, pltpu.roll(re, 64, 1), im))
    packed = jnp.concatenate(rows, axis=0).astype(jnp.bfloat16)
    out_ref[...] = jnp.broadcast_to(packed[None], out_ref.shape)


def source_rows(parts, table, after):
    return pl.pallas_call(
        source_body,
        out_shape=jax.ShapeDtypeStruct((parts.shape[0], GROUPS, 128), jnp.bfloat16),
        in_specs=[pl.BlockSpec(memory_space=pltpu.VMEM)] * 2 + [pl.BlockSpec(memory_space=pl.ANY)],
        out_specs=pl.BlockSpec(memory_space=pltpu.VMEM),
        compiler_params=pltpu.CompilerParams(vmem_limit_bytes=SOURCE_VMEM),
        cost_estimate=pl.CostEstimate(flops=2 * 8 * 1024 * 1024, bytes_accessed=3 * 10**6, transcendentals=0),
        name="source_rows",
    )(parts, table, after)


def whiten_body(raw_ref, half_ref, out_ref, done_ref, spec_ref, amp_ref, table_ref):
    @pl.when(pl.program_id(0) == 0)
    def _():
        row = lax.broadcasted_iota(jnp.int32, half_ref.shape, 0)
        part = half_ref[...]
        table_ref[:, : SEGLEN // 2] = part
        table_ref[:, SEGLEN // 2 :] = jnp.where(row % 2 == 0, -part, part)

    count = raw_ref.shape[1]
    width = 2 * count
    step = 32
    size = step + 16
    zero = jnp.zeros((8, width), jnp.float32)
    amp_ref[0:8, :] = zero
    amp_ref[FREQS + 8 : FREQS + 16, :] = zero
    spec_ref[...] = nt_dot(table_ref[...], raw_ref[...].reshape(width, SEGLEN))
    level = zero
    for f in range(0, FREQS, step):
        real = spec_ref[f : f + step, :]
        imag = spec_ref[FREQS + f : FREQS + f + step, :]
        amplitude = jnp.sqrt(real * real + imag * imag)
        amp_ref[8 + f : 8 + f + step, :] = amplitude
        for i in range(0, step, 8):
            level += amplitude[i : i + 8]
    level = jnp.sum(level, axis=0, keepdims=True) * (WATER / FREQS) + EPS
    for f in range(0, FREQS, step):
        a = amp_ref[f : f + size, :]
        s2 = a + pltpu.roll(a, size - 1, 0)
        s4 = s2 + pltpu.roll(s2, size - 2, 0)
        s9 = s4 + pltpu.roll(s4, 4, 0) + pltpu.roll(a, size - 4, 0)
        inverse = 1.0 / (s9[8 : 8 + step] * (1.0 / (2 * SMOOTH + 1)) + level)
        real = spec_ref[f : f + step, :] * inverse
        imag = spec_ref[FREQS + f : FREQS + f + step, :] * inverse
        for part, value in ((0, real), (1, imag)):
            for i in range(0, step, 8):
                both = jnp.concatenate([value[i : i + 8, :count], value[i : i + 8, count:]], axis=0)
                out_ref[(f + i) // 8, part, 0] = both.astype(jnp.bfloat16)


def whiten(raw, table, half):
    segs, count, length = raw.shape
    pairs = segs // 4
    out, done = pl.pallas_call(
        whiten_body,
        grid=(pairs,),
        in_specs=[
            pl.BlockSpec((2, count, length), lambda i: (i + half * pairs, 0, 0)),
            pl.BlockSpec((2 * FREQS, length // 2), lambda i: (0, 0)),
        ],
        out_specs=[
            pl.BlockSpec((GROUPS, 2, 1, 16, count), lambda i: (0, 0, i, 0, 0)),
            pl.BlockSpec(memory_space=pl.ANY),
        ],
        out_shape=[
            jax.ShapeDtypeStruct((GROUPS, 2, pairs, 16, count), jnp.bfloat16),
            jax.ShapeDtypeStruct((8, 128), jnp.float32),
        ],
        scratch_shapes=[
            pltpu.VMEM((2 * FREQS, 2 * count), jnp.float32),
            pltpu.VMEM((FREQS + 16, 2 * count), jnp.float32),
            pltpu.VMEM((2 * FREQS, length), jnp.bfloat16),
        ],
        compiler_params=pltpu.CompilerParams(vmem_limit_bytes=WHITEN_VMEM),
        cost_estimate=pl.CostEstimate(
            flops=2 * 1024 * 1024 * 1024, bytes_accessed=6 * 10**6, transcendentals=10**6
        ),
        name=f"whiten{half}",
    )(raw, table)
    return out.reshape(GROUPS, 32 * pairs, count), done


def correlate_body(src_ref, w0_ref, w1_ref, lag_ref, *refs):
    out_refs = refs[:4]
    s_ref, w_ref, table_ref, high_ref, low_ref, sum_ref, sems, table_sem = refs[4:]
    count = w0_ref.shape[2]
    deep = w0_ref.shape[1]
    parts = len(PARTS) - 1

    def load(i, half):
        at = pl.ds(PARTS[i], PARTS[i + 1] - PARTS[i])
        source = (w0_ref, w1_ref)[half]
        return pltpu.make_async_copy(
            source.at[at], w_ref.at[at, pl.ds(half * deep, deep)], sems.at[i, half]
        )

    for i in range(parts):
        load(i, 0).start()
        load(i, 1).start()
    table_copy = pltpu.make_async_copy(lag_ref, table_ref, table_sem)
    table_copy.start()

    lanes = lax.broadcasted_iota(jnp.int32, (GROUPS, 128), 1)
    for i in range(2 * SOURCES):
        value = src_ref[i].astype(jnp.float32)
        s_ref[0, i] = value
        turned = pltpu.roll(value, 64, 1)
        s_ref[1, i] = jnp.where(lanes < 64, -turned, turned)

    sub = lax.broadcasted_iota(jnp.int32, (8, 128), 0)
    lane = lax.broadcasted_iota(jnp.int32, (8, 128), 1)
    diagonal = (lane % 8) == sub

    def cross(b):
        tiles = []
        for q in range(SOURCES):
            halves = []
            for h in range(2):
                pieces = []
                for r in range(2):
                    row = jnp.broadcast_to(s_ref[r, 2 * q + h, b : b + 1, :], (8, 128))
                    pieces.append(jnp.where(diagonal, row, 0.0))
                halves.append(jnp.concatenate(pieces, axis=0).astype(jnp.bfloat16))
            tiles.append(jnp.concatenate(halves, axis=1))
        return nn_dot(jnp.concatenate(tiles, axis=0), w_ref[b])

    def turn(x):
        x = x.reshape(LAG_ROWS // 8, 8, x.shape[1])[: HALFLAG // 8 + 1]
        row = lax.broadcasted_iota(jnp.int32, x.shape, 1)
        even = jnp.where(row % 4 == 0, x, pltpu.roll(x, 4, 1))
        odd = jnp.where(row % 4 == 1, pltpu.roll(x, 2, 1), pltpu.roll(x, 6, 1))
        x = jnp.where(row % 2 == 0, even, odd)
        groups = []
        for j in range(HALFLAG // 8):
            groups.append(jnp.where(row[0] == 0, x[HALFLAG // 8 - j], x[HALFLAG // 8 - 1 - j]))
        return jnp.concatenate(groups, axis=0)

    def chunk(i):
        load(i, 0).wait()
        load(i, 1).wait()
        for b in range(PARTS[i], PARTS[i + 1], 2):
            one, two = cross(b), cross(b + 1)
            at = slice(b * 8, b * 8 + 16)
            for q in range(SOURCES):
                cols = slice((q % 2) * count, (q % 2 + 1) * count)
                for r in range(2):
                    rows = slice(q * 16 + r * 8, q * 16 + r * 8 + 8)
                    both = jnp.concatenate([one[rows], two[rows]], axis=0)
                    high = both.astype(jnp.bfloat16)
                    high_ref[q // 2, r, at, cols] = high
                    low_ref[q // 2, r, at, cols] = (both - high.astype(jnp.float32)).astype(jnp.bfloat16)

    for i in range(parts):
        chunk(i)
    table_copy.wait()
    me = lax.axis_index("seg")
    share = count // 4
    for p in range(SOURCES // 2):
        terms = []
        for r in range(2):
            first = nn_dot(table_ref[r], high_ref[p, r])
            second = nn_dot(table_ref[r, :LAG_ROWS, :], low_ref[p, r])
            terms.append(first[:LAG_ROWS] + (first[LAG_ROWS:] + second))
        later = terms[0][:HALFLAG] + terms[1][:HALFLAG]
        total = jnp.concatenate([turn(terms[0] - terms[1]), later], axis=0)
        for i in range(2):
            sum_ref[2 * p + i] = total[:, i * count : (i + 1) * count].T

    def part(r):
        return sum_ref[:, pl.ds(pl.multiple_of((me ^ r) * share, share), share), :]

    for r, out_ref in enumerate(out_refs):
        out_ref[...] = part(r)


def correlate(src, w0, w1, lag):
    count = w0.shape[2]
    parts = len(PARTS) - 1
    share = count // 4
    shape = (SOURCES, share, LAGS)
    vmem = pl.BlockSpec(memory_space=pltpu.VMEM)
    anywhere = pl.BlockSpec(memory_space=pl.ANY)
    return pl.pallas_call(
        correlate_body,
        in_specs=[vmem, anywhere, anywhere, anywhere],
        out_specs=[vmem] * 4,
        out_shape=[jax.ShapeDtypeStruct(shape, jnp.float32)] * 4,
        scratch_shapes=[
            pltpu.VMEM((2, 2 * SOURCES, GROUPS, 128), jnp.float32),
            pltpu.VMEM((GROUPS, 2 * w0.shape[1], count), jnp.bfloat16),
            pltpu.VMEM(lag.shape, lag.dtype),
            pltpu.VMEM((SOURCES // 2, 2, FREQS, 2 * count), jnp.bfloat16),
            pltpu.VMEM((SOURCES // 2, 2, FREQS, 2 * count), jnp.bfloat16),
            pltpu.VMEM((SOURCES, count, LAGS), jnp.float32),
            pltpu.SemaphoreType.DMA((parts, 2)),
            pltpu.SemaphoreType.DMA,
        ],
        compiler_params=pltpu.CompilerParams(vmem_limit_bytes=CORRELATE_VMEM),
        cost_estimate=pl.CostEstimate(flops=3 * 10**9, bytes_accessed=6 * 10**6, transcendentals=0),
        name="correlate",
    )(src, w0, w1, lag)


def chip_sum_body(mine_ref, core_ref, out_ref):
    out_ref[...] = (mine_ref[...] + core_ref[...]).astype(jnp.bfloat16)


def chip_sum(mine, core):
    return pl.pallas_call(
        chip_sum_body,
        in_specs=[pl.BlockSpec(memory_space=pltpu.VMEM)] * 2,
        out_specs=pl.BlockSpec(memory_space=pltpu.VMEM),
        out_shape=jax.ShapeDtypeStruct(mine.shape, jnp.bfloat16),
        compiler_params=pltpu.CompilerParams(vmem_limit_bytes=SUM_VMEM),
        cost_estimate=pl.CostEstimate(flops=10**5, bytes_accessed=10**6, transcendentals=0),
        name="chip_sum",
    )(mine, core)


def gather_sum_body(mine_ref, core_ref, far_ref, out_ref):
    total = (mine_ref[...] + core_ref[...]) + far_ref[...].astype(jnp.float32)
    for q in range(SOURCES):
        out_ref[:, q, :] = total[q]


def gather_sum(mine, core, far):
    shape = mine.shape
    return pl.pallas_call(
        gather_sum_body,
        in_specs=[pl.BlockSpec(memory_space=pltpu.VMEM)] * 3,
        out_specs=pl.BlockSpec(memory_space=pltpu.VMEM),
        out_shape=jax.ShapeDtypeStruct((shape[1], shape[0], shape[2]), jnp.float32),
        compiler_params=pltpu.CompilerParams(vmem_limit_bytes=SUM_VMEM),
        cost_estimate=pl.CostEstimate(flops=10**6, bytes_accessed=10**6, transcendentals=0),
        name="gather_sum",
    )(mine, core, far)


def local(raw, source_index, source_block):
    segs = raw.shape[0] * lax.axis_size("seg")
    ways = lax.axis_size("ch")
    table = jnp.asarray(dft_rows())
    lag = jnp.asarray(lag_rows(1.0 / (FREQS * segs)))
    picked = pick(raw, source_index, source_block)
    parts = lax.all_to_all(picked.reshape(ways, 8, SEGLEN), "ch", 0, 0)
    w0, done = whiten(raw, table, 0)
    spread = source_rows(parts, table, done)
    src = lax.all_to_all(spread, "ch", 0, 0)
    w1, _ = whiten(raw, table, 1)
    parts = correlate(src, w0, w1, lag)

    def swap(x, r):
        return lax.ppermute(x, "seg", [(i, i ^ r) for i in range(4)])

    far = swap(chip_sum(parts[2], swap(parts[3], 1)), 2)
    return gather_sum(parts[0], swap(parts[1], 1), far)


def solution(mesh):
    return jax.shard_map(
        local,
        mesh=mesh,
        in_specs=(P("seg", "ch", None), P(), P()),
        out_specs=P(("ch", "seg"), None, None),
        check_vma=False,
    )
```

```python
import functools

import jax
import jax.numpy as jnp
import ml_dtypes
import numpy as np
from jax import lax
from jax.experimental import pallas as pl
from jax.experimental.pallas import tpu as pltpu
from jax.sharding import PartitionSpec as P

SEGLEN = 1024
FREQS = 512
HALFLAG = 64
LAGS = 128
SMOOTH = 4
SOURCES = 16
PER_BLOCK = 4
WATER = 0.1
EPS = 1e-06

GROUPS = FREQS // 8
ROWS = 16
LAG_ROWS = 80
PARTS = (0, 8, 32, 64)
PICK_VMEM = 58 << 20
WHITEN_VMEM = 52 << 20
SOURCE_VMEM = 48 << 20
CORRELATE_VMEM = 52 << 20
SUM_VMEM = 14 << 20


def dft_rows():
    bins = np.arange(1, FREQS + 1)[:, None]
    times = np.arange(SEGLEN)[None, :]
    phase = ((bins * times) % SEGLEN).astype(np.float32) * np.float32(2.0 * np.pi / SEGLEN)
    table = np.concatenate([np.cos(phase), -np.sin(phase)], axis=0)
    return table.astype(ml_dtypes.bfloat16)


def lag_rows(scale):
    bins = np.arange(1, FREQS + 1)[None, :]
    lags = np.arange(LAG_ROWS)[:, None]
    theta = ((bins * lags) % SEGLEN).astype(np.float32) * np.float32(2.0 * np.pi / SEGLEN)
    table = np.stack([np.cos(theta), np.sin(theta)]) * np.float32(scale)
    table = np.where(lags[None] <= HALFLAG, table, np.float32(0.0)).astype(np.float32)
    high = table.astype(ml_dtypes.bfloat16)
    low = (table - high.astype(np.float32)).astype(ml_dtypes.bfloat16)
    return np.concatenate([high, low], axis=1)


def nt_dot(a, b):
    return lax.dot_general(a, b, (((1,), (1,)), ((), ())), preferred_element_type=jnp.float32)


def nn_dot(a, b):
    return lax.dot_general(a, b, (((1,), (0,)), ((), ())), preferred_element_type=jnp.float32)


def pick_body(index_ref, block_ref, raw_ref, out_ref, chan_ref, own_ref, held_ref, got_ref, zero_ref, sems, out_sems):
    segs, count, _ = raw_ref.shape
    first = lax.axis_index("ch") * count

    def load(q):
        start = pl.multiple_of(jnp.clip(chan_ref[q], 0, count - 1) // ROWS * ROWS, ROWS)
        return pltpu.make_async_copy(raw_ref.at[:, pl.ds(start, ROWS)], held_ref.at[q], sems.at[q])

    def store(q, source):
        return pltpu.make_async_copy(source, out_ref.at[q], out_sems.at[q])

    zero_ref[...] = jnp.zeros_like(zero_ref)
    held = jnp.int32(0)
    for s in range(SOURCES):
        rank = jnp.int32(0)
        for t in range(s):
            rank += jnp.where(block_ref[t] == block_ref[s], 1, 0).astype(jnp.int32)
        q = block_ref[s] * PER_BLOCK + rank
        chan = index_ref[s] - first
        chan_ref[q] = chan
        ours = (chan >= 0) & (chan < count)
        own_ref[held] = q
        held += jnp.where(ours, 1, 0).astype(jnp.int32)

        @pl.when(ours)
        def _(q=q):
            load(q).start()

        @pl.when(jnp.logical_not(ours))
        def _(q=q):
            store(q, zero_ref).start()

    row = lax.broadcasted_iota(jnp.int32, (segs, segs * ROWS), 0)
    column = lax.broadcasted_iota(jnp.int32, (segs, segs * ROWS), 1)

    def two(i, carry):
        qs = (own_ref[2 * i], own_ref[jnp.minimum(2 * i + 1, held - 1)])
        more = 2 * i + 1 < held
        load(qs[0]).wait()

        @pl.when(more)
        def _():
            load(qs[1]).wait()

        gots = []
        for q in qs:
            hit = column == row * ROWS + chan_ref[q] % ROWS
            rows = held_ref[q].reshape(segs * ROWS, SEGLEN)
            gots.append(nn_dot(jnp.where(hit, 1.0, 0.0).astype(jnp.bfloat16), rows))
        for k, got in enumerate(gots):
            got_ref[2 * i + k] = got.astype(jnp.bfloat16).reshape(segs // 8, 8, SEGLEN)
        store(qs[0], got_ref.at[2 * i]).start()

        @pl.when(more)
        def _():
            store(qs[1], got_ref.at[2 * i + 1]).start()

        return carry

    lax.fori_loop(0, (held + 1) // 2, two, 0)
    for q in range(SOURCES):
        store(q, zero_ref).wait()


def pick(raw, source_index, source_block):
    segs, count, length = raw.shape
    shape = (segs // 8, 8, length)
    return pl.pallas_call(
        pick_body,
        grid_spec=pltpu.PrefetchScalarGridSpec(
            num_scalar_prefetch=2,
            grid=(1,),
            in_specs=[pl.BlockSpec(memory_space=pl.ANY)],
            out_specs=pl.BlockSpec(memory_space=pl.ANY),
            scratch_shapes=[
                pltpu.SMEM((SOURCES,), jnp.int32),
                pltpu.SMEM((SOURCES,), jnp.int32),
                pltpu.VMEM((SOURCES, segs, ROWS, length), raw.dtype),
                pltpu.VMEM((SOURCES, *shape), raw.dtype),
                pltpu.VMEM(shape, raw.dtype),
                pltpu.SemaphoreType.DMA((SOURCES,)),
                pltpu.SemaphoreType.DMA((SOURCES,)),
            ],
        ),
        out_shape=jax.ShapeDtypeStruct((SOURCES, *shape), jnp.bfloat16),
        compiler_params=pltpu.CompilerParams(vmem_limit_bytes=PICK_VMEM),
        cost_estimate=pl.CostEstimate(flops=10**8, bytes_accessed=3 * 10**6, transcendentals=0),
        name="pick",
    )(source_index, source_block, raw)


def source_body(parts_ref, table_ref, after_ref, out_ref, tile_ref, sems):
    total = jnp.sum(parts_ref[...].astype(jnp.float32), axis=0)
    spectrum = nt_dot(total.astype(jnp.bfloat16), table_ref[...])
    real = spectrum[:, :FREQS]
    imag = spectrum[:, FREQS:]
    amplitude = jnp.sqrt(real * real + imag * imag)
    place = lax.broadcasted_iota(jnp.int32, amplitude.shape, 1)
    smoothed = amplitude
    for shift in range(1, SMOOTH + 1):
        later = pltpu.roll(amplitude, FREQS - shift, 1)
        smoothed += jnp.where(place < FREQS - shift, later, 0.0)
        earlier = pltpu.roll(amplitude, shift, 1)
        smoothed += jnp.where(place >= shift, earlier, 0.0)
    level = jnp.sum(amplitude, axis=1, keepdims=True) * (1.0 / FREQS)
    divisor = smoothed / (2 * SMOOTH + 1) + WATER * level + EPS
    real = (real / divisor).astype(jnp.bfloat16).astype(jnp.float32)
    imag = (imag / divisor).astype(jnp.bfloat16).astype(jnp.float32)
    sub = lax.broadcasted_iota(jnp.int32, (8, 128), 0)
    lane = lax.broadcasted_iota(jnp.int32, (8, 128), 1)
    block = (lane // 8) % 8

    def turn(x):
        for s in (4, 2, 1):
            down = pltpu.roll(pltpu.roll(x, s, 0), 128 - 8 * s, 1)
            up = pltpu.roll(pltpu.roll(x, 8 - s, 0), 8 * s, 1)
            low_row = (sub & s) == 0
            low_block = (block & s) == 0
            x = jnp.where(low_row == low_block, x, jnp.where(low_row, up, down))
        return x

    rows = []
    for j in range(FREQS // 128):
        re = turn(real[:, j * 128 : (j + 1) * 128])
        im = turn(imag[:, j * 128 : (j + 1) * 128])
        rows.append(jnp.where(lane < 64, re, pltpu.roll(im, 64, 1)))
        rows.append(jnp.where(lane < 64, pltpu.roll(re, 64, 1), im))
    packed = jnp.concatenate(rows, axis=0).astype(jnp.bfloat16)
    tile_ref[...] = jnp.broadcast_to(packed[None], tile_ref.shape)
    size = tile_ref.shape[0]
    copies = []
    for i in range(out_ref.shape[0] // size):
        copies.append(pltpu.make_async_copy(tile_ref, out_ref.at[pl.ds(i * size, size)], sems.at[i]))
        copies[-1].start()
    for copy in copies:
        copy.wait()


def source_rows(parts, table, after):
    return pl.pallas_call(
        source_body,
        out_shape=jax.ShapeDtypeStruct((parts.shape[0], GROUPS, 128), jnp.bfloat16),
        in_specs=[pl.BlockSpec(memory_space=pltpu.VMEM)] * 2 + [pl.BlockSpec(memory_space=pl.ANY)],
        out_specs=pl.BlockSpec(memory_space=pl.ANY),
        scratch_shapes=[
            pltpu.VMEM((parts.shape[0] // 4, GROUPS, 128), jnp.bfloat16),
            pltpu.SemaphoreType.DMA((4,)),
        ],
        compiler_params=pltpu.CompilerParams(vmem_limit_bytes=SOURCE_VMEM),
        cost_estimate=pl.CostEstimate(flops=2 * 8 * 1024 * 1024, bytes_accessed=3 * 10**6, transcendentals=0),
        name="source_rows",
    )(parts, table, after)


def whiten_body(raw_ref, half_ref, out_ref, done_ref, spec_ref, amp_ref, table_ref):
    @pl.when(pl.program_id(0) == 0)
    def _():
        row = lax.broadcasted_iota(jnp.int32, half_ref.shape, 0)
        part = half_ref[...]
        table_ref[:, : SEGLEN // 2] = part
        table_ref[:, SEGLEN // 2 :] = jnp.where(row % 2 == 0, -part, part)

    count = raw_ref.shape[1]
    width = 2 * count
    step = 32
    size = step + 16
    zero = jnp.zeros((8, width), jnp.float32)
    amp_ref[0:8, :] = zero
    amp_ref[FREQS + 8 : FREQS + 16, :] = zero
    spec_ref[...] = nt_dot(table_ref[...], raw_ref[...].reshape(width, SEGLEN))
    level = zero
    for f in range(0, FREQS, step):
        real = spec_ref[f : f + step, :]
        imag = spec_ref[FREQS + f : FREQS + f + step, :]
        amplitude = jnp.sqrt(real * real + imag * imag)
        amp_ref[8 + f : 8 + f + step, :] = amplitude
        for i in range(0, step, 8):
            level += amplitude[i : i + 8]
    level = jnp.sum(level, axis=0, keepdims=True) * (WATER / FREQS) + EPS
    for f in range(0, FREQS, step):
        a = amp_ref[f : f + size, :]
        s2 = a + pltpu.roll(a, size - 1, 0)
        s4 = s2 + pltpu.roll(s2, size - 2, 0)
        s9 = s4 + pltpu.roll(s4, 4, 0) + pltpu.roll(a, size - 4, 0)
        inverse = 1.0 / (s9[8 : 8 + step] * (1.0 / (2 * SMOOTH + 1)) + level)
        real = spec_ref[f : f + step, :] * inverse
        imag = spec_ref[FREQS + f : FREQS + f + step, :] * inverse
        for part, value in ((0, real), (1, imag)):
            for i in range(0, step, 8):
                both = jnp.concatenate([value[i : i + 8, :count], value[i : i + 8, count:]], axis=0)
                out_ref[(f + i) // 8, part, 0] = both.astype(jnp.bfloat16)


def whiten(raw, table, half):
    segs, count, length = raw.shape
    pairs = segs // 4
    out, done = pl.pallas_call(
        whiten_body,
        grid=(pairs,),
        in_specs=[
            pl.BlockSpec((2, count, length), lambda i: (i + half * pairs, 0, 0)),
            pl.BlockSpec((2 * FREQS, length // 2), lambda i: (0, 0)),
        ],
        out_specs=[
            pl.BlockSpec((GROUPS, 2, 1, 16, count), lambda i: (0, 0, i, 0, 0)),
            pl.BlockSpec(memory_space=pl.ANY),
        ],
        out_shape=[
            jax.ShapeDtypeStruct((GROUPS, 2, pairs, 16, count), jnp.bfloat16),
            jax.ShapeDtypeStruct((8, 128), jnp.float32),
        ],
        scratch_shapes=[
            pltpu.VMEM((2 * FREQS, 2 * count), jnp.float32),
            pltpu.VMEM((FREQS + 16, 2 * count), jnp.float32),
            pltpu.VMEM((2 * FREQS, length), jnp.bfloat16),
        ],
        compiler_params=pltpu.CompilerParams(vmem_limit_bytes=WHITEN_VMEM),
        cost_estimate=pl.CostEstimate(
            flops=2 * 1024 * 1024 * 1024, bytes_accessed=6 * 10**6, transcendentals=10**6
        ),
        name=f"whiten{half}",
    )(raw, table)
    return out.reshape(GROUPS, 32 * pairs, count), done


def correlate_body(src_ref, w0_ref, w1_ref, lag_ref, *refs):
    out_refs = refs[:4]
    s_ref, w_ref, table_ref, high_ref, low_ref, sum_ref, sems, table_sem = refs[4:]
    count = w0_ref.shape[2]
    deep = w0_ref.shape[1]
    parts = len(PARTS) - 1

    def load(i, half):
        at = pl.ds(PARTS[i], PARTS[i + 1] - PARTS[i])
        source = (w0_ref, w1_ref)[half]
        return pltpu.make_async_copy(
            source.at[at], w_ref.at[at, pl.ds(half * deep, deep)], sems.at[i, half]
        )

    for i in range(parts):
        load(i, 0).start()
        load(i, 1).start()
    table_copy = pltpu.make_async_copy(lag_ref, table_ref, table_sem)
    table_copy.start()

    lanes = lax.broadcasted_iota(jnp.int32, (GROUPS, 128), 1)
    for i in range(2 * SOURCES):
        value = src_ref[i].astype(jnp.float32)
        s_ref[0, i] = value
        turned = pltpu.roll(value, 64, 1)
        s_ref[1, i] = jnp.where(lanes < 64, -turned, turned)

    sub = lax.broadcasted_iota(jnp.int32, (8, 128), 0)
    lane = lax.broadcasted_iota(jnp.int32, (8, 128), 1)
    diagonal = (lane % 8) == sub

    def cross(b):
        tiles = []
        for q in range(SOURCES):
            halves = []
            for h in range(2):
                pieces = []
                for r in range(2):
                    row = jnp.broadcast_to(s_ref[r, 2 * q + h, b : b + 1, :], (8, 128))
                    pieces.append(jnp.where(diagonal, row, 0.0))
                halves.append(jnp.concatenate(pieces, axis=0).astype(jnp.bfloat16))
            tiles.append(jnp.concatenate(halves, axis=1))
        return nn_dot(jnp.concatenate(tiles, axis=0), w_ref[b])

    def turn(x):
        x = x.reshape(LAG_ROWS // 8, 8, x.shape[1])[: HALFLAG // 8 + 1]
        row = lax.broadcasted_iota(jnp.int32, x.shape, 1)
        even = jnp.where(row % 4 == 0, x, pltpu.roll(x, 4, 1))
        odd = jnp.where(row % 4 == 1, pltpu.roll(x, 2, 1), pltpu.roll(x, 6, 1))
        x = jnp.where(row % 2 == 0, even, odd)
        groups = []
        for j in range(HALFLAG // 8):
            groups.append(jnp.where(row[0] == 0, x[HALFLAG // 8 - j], x[HALFLAG // 8 - 1 - j]))
        return jnp.concatenate(groups, axis=0)

    def chunk(i):
        load(i, 0).wait()
        load(i, 1).wait()
        for b in range(PARTS[i], PARTS[i + 1], 2):
            one, two = cross(b), cross(b + 1)
            at = slice(b * 8, b * 8 + 16)
            for q in range(SOURCES):
                cols = slice((q % 2) * count, (q % 2 + 1) * count)
                for r in range(2):
                    rows = slice(q * 16 + r * 8, q * 16 + r * 8 + 8)
                    both = jnp.concatenate([one[rows], two[rows]], axis=0)
                    high = both.astype(jnp.bfloat16)
                    high_ref[q // 2, r, at, cols] = high
                    low_ref[q // 2, r, at, cols] = (both - high.astype(jnp.float32)).astype(jnp.bfloat16)

    for i in range(parts):
        chunk(i)
    table_copy.wait()
    me = lax.axis_index("seg")
    share = count // 4
    for p in range(SOURCES // 2):
        terms = []
        for r in range(2):
            first = nn_dot(table_ref[r], high_ref[p, r])
            second = nn_dot(table_ref[r, :LAG_ROWS, :], low_ref[p, r])
            terms.append(first[:LAG_ROWS] + (first[LAG_ROWS:] + second))
        later = terms[0][:HALFLAG] + terms[1][:HALFLAG]
        total = jnp.concatenate([turn(terms[0] - terms[1]), later], axis=0)
        for i in range(2):
            sum_ref[2 * p + i] = total[:, i * count : (i + 1) * count].T

    def part(r):
        return sum_ref[:, pl.ds(pl.multiple_of((me ^ r) * share, share), share), :]

    for r, out_ref in enumerate(out_refs):
        out_ref[...] = part(r)


def correlate(src, w0, w1, lag):
    count = w0.shape[2]
    parts = len(PARTS) - 1
    share = count // 4
    shape = (SOURCES, share, LAGS)
    vmem = pl.BlockSpec(memory_space=pltpu.VMEM)
    anywhere = pl.BlockSpec(memory_space=pl.ANY)
    return pl.pallas_call(
        correlate_body,
        in_specs=[vmem, anywhere, anywhere, anywhere],
        out_specs=[vmem] * 4,
        out_shape=[jax.ShapeDtypeStruct(shape, jnp.float32)] * 4,
        scratch_shapes=[
            pltpu.VMEM((2, 2 * SOURCES, GROUPS, 128), jnp.float32),
            pltpu.VMEM((GROUPS, 2 * w0.shape[1], count), jnp.bfloat16),
            pltpu.VMEM(lag.shape, lag.dtype),
            pltpu.VMEM((SOURCES // 2, 2, FREQS, 2 * count), jnp.bfloat16),
            pltpu.VMEM((SOURCES // 2, 2, FREQS, 2 * count), jnp.bfloat16),
            pltpu.VMEM((SOURCES, count, LAGS), jnp.float32),
            pltpu.SemaphoreType.DMA((parts, 2)),
            pltpu.SemaphoreType.DMA,
        ],
        compiler_params=pltpu.CompilerParams(vmem_limit_bytes=CORRELATE_VMEM),
        cost_estimate=pl.CostEstimate(flops=3 * 10**9, bytes_accessed=6 * 10**6, transcendentals=0),
        name="correlate",
    )(src, w0, w1, lag)


def chip_sum_body(mine_ref, core_ref, out_ref):
    out_ref[...] = (mine_ref[...] + core_ref[...]).astype(jnp.bfloat16)


def chip_sum(mine, core):
    return pl.pallas_call(
        chip_sum_body,
        in_specs=[pl.BlockSpec(memory_space=pltpu.VMEM)] * 2,
        out_specs=pl.BlockSpec(memory_space=pltpu.VMEM),
        out_shape=jax.ShapeDtypeStruct(mine.shape, jnp.bfloat16),
        compiler_params=pltpu.CompilerParams(vmem_limit_bytes=SUM_VMEM),
        cost_estimate=pl.CostEstimate(flops=10**5, bytes_accessed=10**6, transcendentals=0),
        name="chip_sum",
    )(mine, core)


def gather_sum_body(mine_ref, core_ref, far_ref, out_ref):
    total = (mine_ref[...] + core_ref[...]) + far_ref[...].astype(jnp.float32)
    for q in range(SOURCES):
        out_ref[:, q, :] = total[q]


def gather_sum(mine, core, far):
    shape = mine.shape
    return pl.pallas_call(
        gather_sum_body,
        in_specs=[pl.BlockSpec(memory_space=pltpu.VMEM)] * 3,
        out_specs=pl.BlockSpec(memory_space=pltpu.VMEM),
        out_shape=jax.ShapeDtypeStruct((shape[1], shape[0], shape[2]), jnp.float32),
        compiler_params=pltpu.CompilerParams(vmem_limit_bytes=SUM_VMEM),
        cost_estimate=pl.CostEstimate(flops=10**6, bytes_accessed=10**6, transcendentals=0),
        name="gather_sum",
    )(mine, core, far)


def local(raw, source_index, source_block):
    segs = raw.shape[0] * lax.axis_size("seg")
    ways = lax.axis_size("ch")
    table = jnp.asarray(dft_rows())
    lag = jnp.asarray(lag_rows(1.0 / (FREQS * segs)))
    picked = pick(raw, source_index, source_block)
    parts = lax.all_to_all(picked.reshape(ways, 8, SEGLEN), "ch", 0, 0)
    w0, done = whiten(raw, table, 0)
    spread = source_rows(parts, table, done)
    src = lax.all_to_all(spread, "ch", 0, 0)
    w1, _ = whiten(raw, table, 1)
    parts = correlate(src, w0, w1, lag)

    def swap(x, r):
        return lax.ppermute(x, "seg", [(i, i ^ r) for i in range(4)])

    far = swap(chip_sum(parts[2], swap(parts[3], 1)), 2)
    return gather_sum(parts[0], swap(parts[1], 1), far)


def solution(mesh):
    return jax.shard_map(
        local,
        mesh=mesh,
        in_specs=(P("seg", "ch", None), P(), P()),
        out_specs=P(("ch", "seg"), None, None),
        check_vma=False,
    )
```

```python
import functools

import jax
import jax.numpy as jnp
import ml_dtypes
import numpy as np
from jax import lax
from jax.experimental import pallas as pl
from jax.experimental.pallas import tpu as pltpu
from jax.sharding import PartitionSpec as P

SEGLEN = 1024
FREQS = 512
HALFLAG = 64
LAGS = 128
SMOOTH = 4
SOURCES = 16
PER_BLOCK = 4
WATER = 0.1
EPS = 1e-06

GROUPS = FREQS // 8
ROWS = 16
LAG_ROWS = 80
PARTS = (0, 8, 32, 64)
PICK_VMEM = 58 << 20
WHITEN_VMEM = 52 << 20
SOURCE_VMEM = 48 << 20
CORRELATE_VMEM = 52 << 20
SUM_VMEM = 14 << 20


def dft_rows():
    bins = np.arange(1, FREQS + 1)[:, None]
    times = np.arange(SEGLEN)[None, :]
    phase = ((bins * times) % SEGLEN).astype(np.float32) * np.float32(2.0 * np.pi / SEGLEN)
    table = np.concatenate([np.cos(phase), -np.sin(phase)], axis=0)
    return table.astype(ml_dtypes.bfloat16)


def lag_rows(scale):
    bins = np.arange(1, FREQS + 1)[None, :]
    lags = np.arange(LAG_ROWS)[:, None]
    theta = ((bins * lags) % SEGLEN).astype(np.float32) * np.float32(2.0 * np.pi / SEGLEN)
    table = np.stack([np.cos(theta), np.sin(theta)]) * np.float32(scale)
    table = np.where(lags[None] <= HALFLAG, table, np.float32(0.0)).astype(np.float32)
    high = table.astype(ml_dtypes.bfloat16)
    low = (table - high.astype(np.float32)).astype(ml_dtypes.bfloat16)
    return np.concatenate([high, low], axis=1)


def nt_dot(a, b):
    return lax.dot_general(a, b, (((1,), (1,)), ((), ())), preferred_element_type=jnp.float32)


def nn_dot(a, b):
    return lax.dot_general(a, b, (((1,), (0,)), ((), ())), preferred_element_type=jnp.float32)


def pick_body(index_ref, block_ref, raw_ref, out_ref, chan_ref, held_ref, got_ref, zero_ref, sems, out_sems):
    segs, count, _ = raw_ref.shape
    first = lax.axis_index("ch") * count
    for s in range(SOURCES):
        rank = jnp.int32(0)
        for t in range(s):
            rank += jnp.where(block_ref[t] == block_ref[s], 1, 0).astype(jnp.int32)
        chan_ref[block_ref[s] * PER_BLOCK + rank] = index_ref[s] - first

    def ours(q):
        return (chan_ref[q] >= 0) & (chan_ref[q] < count)

    def load(q):
        start = pl.multiple_of(jnp.clip(chan_ref[q], 0, count - 1) // ROWS * ROWS, ROWS)
        return pltpu.make_async_copy(raw_ref.at[:, pl.ds(start, ROWS)], held_ref.at[q], sems.at[q])

    def store(q, source):
        return pltpu.make_async_copy(source, out_ref.at[q], out_sems.at[q])

    for q in range(SOURCES):
        pl.when(ours(q))(lambda q=q: load(q).start())
    zero_ref[...] = jnp.zeros_like(zero_ref)
    for q in range(SOURCES):
        pl.when(jnp.logical_not(ours(q)))(lambda q=q: store(q, zero_ref).start())
    row = lax.broadcasted_iota(jnp.int32, (segs, segs * ROWS), 0)
    column = lax.broadcasted_iota(jnp.int32, (segs, segs * ROWS), 1)
    for q in range(SOURCES):

        @pl.when(ours(q))
        def _(q=q):
            load(q).wait()
            hit = column == row * ROWS + chan_ref[q] % ROWS
            rows = held_ref[q].reshape(segs * ROWS, SEGLEN)
            got = nn_dot(jnp.where(hit, 1.0, 0.0).astype(jnp.bfloat16), rows)
            got_ref[q] = got.astype(jnp.bfloat16).reshape(segs // 8, 8, SEGLEN)
            store(q, got_ref.at[q]).start()

    for q in range(SOURCES):
        store(q, zero_ref).wait()


def pick(raw, source_index, source_block):
    segs, count, length = raw.shape
    shape = (segs // 8, 8, length)
    return pl.pallas_call(
        pick_body,
        grid_spec=pltpu.PrefetchScalarGridSpec(
            num_scalar_prefetch=2,
            grid=(1,),
            in_specs=[pl.BlockSpec(memory_space=pl.ANY)],
            out_specs=pl.BlockSpec(memory_space=pl.ANY),
            scratch_shapes=[
                pltpu.SMEM((SOURCES,), jnp.int32),
                pltpu.VMEM((SOURCES, segs, ROWS, length), raw.dtype),
                pltpu.VMEM((SOURCES, *shape), raw.dtype),
                pltpu.VMEM(shape, raw.dtype),
                pltpu.SemaphoreType.DMA((SOURCES,)),
                pltpu.SemaphoreType.DMA((SOURCES,)),
            ],
        ),
        out_shape=jax.ShapeDtypeStruct((SOURCES, *shape), jnp.bfloat16),
        compiler_params=pltpu.CompilerParams(vmem_limit_bytes=PICK_VMEM),
        cost_estimate=pl.CostEstimate(flops=10**8, bytes_accessed=3 * 10**6, transcendentals=0),
        name="pick",
    )(source_index, source_block, raw)


def source_body(parts_ref, table_ref, after_ref, out_ref):
    total = jnp.sum(parts_ref[...].astype(jnp.float32), axis=0)
    spectrum = nt_dot(total.astype(jnp.bfloat16), table_ref[...])
    real = spectrum[:, :FREQS]
    imag = spectrum[:, FREQS:]
    amplitude = jnp.sqrt(real * real + imag * imag)
    place = lax.broadcasted_iota(jnp.int32, amplitude.shape, 1)
    smoothed = amplitude
    for shift in range(1, SMOOTH + 1):
        later = pltpu.roll(amplitude, FREQS - shift, 1)
        smoothed += jnp.where(place < FREQS - shift, later, 0.0)
        earlier = pltpu.roll(amplitude, shift, 1)
        smoothed += jnp.where(place >= shift, earlier, 0.0)
    level = jnp.sum(amplitude, axis=1, keepdims=True) * (1.0 / FREQS)
    divisor = smoothed / (2 * SMOOTH + 1) + WATER * level + EPS
    real = (real / divisor).astype(jnp.bfloat16).astype(jnp.float32)
    imag = (imag / divisor).astype(jnp.bfloat16).astype(jnp.float32)
    sub = lax.broadcasted_iota(jnp.int32, (8, 128), 0)
    lane = lax.broadcasted_iota(jnp.int32, (8, 128), 1)
    block = (lane // 8) % 8

    def turn(x):
        for s in (4, 2, 1):
            down = pltpu.roll(pltpu.roll(x, s, 0), 128 - 8 * s, 1)
            up = pltpu.roll(pltpu.roll(x, 8 - s, 0), 8 * s, 1)
            low_row = (sub & s) == 0
            low_block = (block & s) == 0
            x = jnp.where(low_row == low_block, x, jnp.where(low_row, up, down))
        return x

    rows = []
    for j in range(FREQS // 128):
        re = turn(real[:, j * 128 : (j + 1) * 128])
        im = turn(imag[:, j * 128 : (j + 1) * 128])
        rows.append(jnp.where(lane < 64, re, pltpu.roll(im, 64, 1)))
        rows.append(jnp.where(lane < 64, pltpu.roll(re, 64, 1), im))
    packed = jnp.concatenate(rows, axis=0).astype(jnp.bfloat16)
    out_ref[...] = jnp.broadcast_to(packed[None], out_ref.shape)


def source_rows(parts, table, after):
    return pl.pallas_call(
        source_body,
        out_shape=jax.ShapeDtypeStruct((parts.shape[0], GROUPS, 128), jnp.bfloat16),
        in_specs=[pl.BlockSpec(memory_space=pltpu.VMEM)] * 2 + [pl.BlockSpec(memory_space=pl.ANY)],
        out_specs=pl.BlockSpec(memory_space=pltpu.VMEM),
        compiler_params=pltpu.CompilerParams(vmem_limit_bytes=SOURCE_VMEM),
        cost_estimate=pl.CostEstimate(flops=2 * 8 * 1024 * 1024, bytes_accessed=3 * 10**6, transcendentals=0),
        name="source_rows",
    )(parts, table, after)


def whiten_body(raw_ref, half_ref, out_ref, done_ref, spec_ref, amp_ref, table_ref):
    @pl.when(pl.program_id(0) == 0)
    def _():
        row = lax.broadcasted_iota(jnp.int32, half_ref.shape, 0)
        part = half_ref[...]
        table_ref[:, : SEGLEN // 2] = part
        table_ref[:, SEGLEN // 2 :] = jnp.where(row % 2 == 0, -part, part)

    count = raw_ref.shape[1]
    width = 2 * count
    step = 16
    size = step + 16
    zero = jnp.zeros((8, width), jnp.float32)
    amp_ref[0:8, :] = zero
    amp_ref[FREQS + 8 : FREQS + 16, :] = zero
    spec_ref[...] = nt_dot(table_ref[...], raw_ref[...].reshape(width, SEGLEN))
    level = zero
    for f in range(0, FREQS, step):
        real = spec_ref[f : f + step, :]
        imag = spec_ref[FREQS + f : FREQS + f + step, :]
        amplitude = jnp.sqrt(real * real + imag * imag)
        amp_ref[8 + f : 8 + f + step, :] = amplitude
        for i in range(0, step, 8):
            level += amplitude[i : i + 8]
    level = jnp.sum(level, axis=0, keepdims=True) * (WATER / FREQS) + EPS
    for f in range(0, FREQS, step):
        a = amp_ref[f : f + size, :]
        s2 = a + pltpu.roll(a, size - 1, 0)
        s4 = s2 + pltpu.roll(s2, size - 2, 0)
        s9 = s4 + pltpu.roll(s4, 4, 0) + pltpu.roll(a, size - 4, 0)
        inverse = 1.0 / (s9[8 : 8 + step] * (1.0 / (2 * SMOOTH + 1)) + level)
        real = spec_ref[f : f + step, :] * inverse
        imag = spec_ref[FREQS + f : FREQS + f + step, :] * inverse
        for part, value in ((0, real), (1, imag)):
            for i in range(0, step, 8):
                both = jnp.concatenate([value[i : i + 8, :count], value[i : i + 8, count:]], axis=0)
                out_ref[(f + i) // 8, part, 0] = both.astype(jnp.bfloat16)


def whiten(raw, table, half):
    segs, count, length = raw.shape
    pairs = segs // 4
    out, done = pl.pallas_call(
        whiten_body,
        grid=(pairs,),
        in_specs=[
            pl.BlockSpec((2, count, length), lambda i: (i + half * pairs, 0, 0)),
            pl.BlockSpec((2 * FREQS, length // 2), lambda i: (0, 0)),
        ],
        out_specs=[
            pl.BlockSpec((GROUPS, 2, 1, 16, count), lambda i: (0, 0, i, 0, 0)),
            pl.BlockSpec(memory_space=pl.ANY),
        ],
        out_shape=[
            jax.ShapeDtypeStruct((GROUPS, 2, pairs, 16, count), jnp.bfloat16),
            jax.ShapeDtypeStruct((8, 128), jnp.float32),
        ],
        scratch_shapes=[
            pltpu.VMEM((2 * FREQS, 2 * count), jnp.float32),
            pltpu.VMEM((FREQS + 16, 2 * count), jnp.float32),
            pltpu.VMEM((2 * FREQS, length), jnp.bfloat16),
        ],
        compiler_params=pltpu.CompilerParams(vmem_limit_bytes=WHITEN_VMEM),
        cost_estimate=pl.CostEstimate(
            flops=2 * 1024 * 1024 * 1024, bytes_accessed=6 * 10**6, transcendentals=10**6
        ),
        name=f"whiten{half}",
    )(raw, table)
    return out.reshape(GROUPS, 32 * pairs, count), done


def correlate_body(src_ref, w0_ref, w1_ref, lag_ref, *refs):
    out_refs = refs[:4]
    s_ref, w_ref, table_ref, high_ref, low_ref, sum_ref, sems, table_sem = refs[4:]
    count = w0_ref.shape[2]
    deep = w0_ref.shape[1]
    parts = len(PARTS) - 1

    def load(i, half):
        at = pl.ds(PARTS[i], PARTS[i + 1] - PARTS[i])
        source = (w0_ref, w1_ref)[half]
        return pltpu.make_async_copy(
            source.at[at], w_ref.at[at, pl.ds(half * deep, deep)], sems.at[i, half]
        )

    for i in range(parts):
        load(i, 0).start()
        load(i, 1).start()
    table_copy = pltpu.make_async_copy(lag_ref, table_ref, table_sem)
    table_copy.start()

    lanes = lax.broadcasted_iota(jnp.int32, (GROUPS, 128), 1)
    for i in range(2 * SOURCES):
        value = src_ref[i].astype(jnp.float32)
        s_ref[0, i] = value
        turned = pltpu.roll(value, 64, 1)
        s_ref[1, i] = jnp.where(lanes < 64, -turned, turned)

    sub = lax.broadcasted_iota(jnp.int32, (8, 128), 0)
    lane = lax.broadcasted_iota(jnp.int32, (8, 128), 1)
    diagonal = (lane % 8) == sub

    def cross(b):
        tiles = []
        for q in range(SOURCES):
            halves = []
            for h in range(2):
                pieces = []
                for r in range(2):
                    row = jnp.broadcast_to(s_ref[r, 2 * q + h, b : b + 1, :], (8, 128))
                    pieces.append(jnp.where(diagonal, row, 0.0))
                halves.append(jnp.concatenate(pieces, axis=0).astype(jnp.bfloat16))
            tiles.append(jnp.concatenate(halves, axis=1))
        return nn_dot(jnp.concatenate(tiles, axis=0), w_ref[b])

    def turn(x):
        x = x.reshape(LAG_ROWS // 8, 8, x.shape[1])[: HALFLAG // 8 + 1]
        row = lax.broadcasted_iota(jnp.int32, x.shape, 1)
        even = jnp.where(row % 4 == 0, x, pltpu.roll(x, 4, 1))
        odd = jnp.where(row % 4 == 1, pltpu.roll(x, 2, 1), pltpu.roll(x, 6, 1))
        x = jnp.where(row % 2 == 0, even, odd)
        groups = []
        for j in range(HALFLAG // 8):
            groups.append(jnp.where(row[0] == 0, x[HALFLAG // 8 - j], x[HALFLAG // 8 - 1 - j]))
        return jnp.concatenate(groups, axis=0)

    def chunk(i):
        load(i, 0).wait()
        load(i, 1).wait()
        for b in range(PARTS[i], PARTS[i + 1], 2):
            one, two = cross(b), cross(b + 1)
            at = slice(b * 8, b * 8 + 16)
            for q in range(SOURCES):
                cols = slice((q % 2) * count, (q % 2 + 1) * count)
                for r in range(2):
                    rows = slice(q * 16 + r * 8, q * 16 + r * 8 + 8)
                    both = jnp.concatenate([one[rows], two[rows]], axis=0)
                    high = both.astype(jnp.bfloat16)
                    high_ref[q // 2, r, at, cols] = high
                    low_ref[q // 2, r, at, cols] = (both - high.astype(jnp.float32)).astype(jnp.bfloat16)

    for i in range(parts):
        chunk(i)
    table_copy.wait()
    me = lax.axis_index("seg")
    share = count // 4
    for p in range(SOURCES // 2):
        terms = []
        for r in range(2):
            first = nn_dot(table_ref[r], high_ref[p, r])
            second = nn_dot(table_ref[r, :LAG_ROWS, :], low_ref[p, r])
            terms.append(first[:LAG_ROWS] + (first[LAG_ROWS:] + second))
        later = terms[0][:HALFLAG] + terms[1][:HALFLAG]
        total = jnp.concatenate([turn(terms[0] - terms[1]), later], axis=0)
        for i in range(2):
            sum_ref[2 * p + i] = total[:, i * count : (i + 1) * count].T

    def part(r):
        return sum_ref[:, pl.ds(pl.multiple_of((me ^ r) * share, share), share), :]

    for r, out_ref in enumerate(out_refs):
        out_ref[...] = part(r)


def correlate(src, w0, w1, lag):
    count = w0.shape[2]
    parts = len(PARTS) - 1
    share = count // 4
    shape = (SOURCES, share, LAGS)
    vmem = pl.BlockSpec(memory_space=pltpu.VMEM)
    anywhere = pl.BlockSpec(memory_space=pl.ANY)
    return pl.pallas_call(
        correlate_body,
        in_specs=[vmem, anywhere, anywhere, anywhere],
        out_specs=[vmem] * 4,
        out_shape=[jax.ShapeDtypeStruct(shape, jnp.float32)] * 4,
        scratch_shapes=[
            pltpu.VMEM((2, 2 * SOURCES, GROUPS, 128), jnp.float32),
            pltpu.VMEM((GROUPS, 2 * w0.shape[1], count), jnp.bfloat16),
            pltpu.VMEM(lag.shape, lag.dtype),
            pltpu.VMEM((SOURCES // 2, 2, FREQS, 2 * count), jnp.bfloat16),
            pltpu.VMEM((SOURCES // 2, 2, FREQS, 2 * count), jnp.bfloat16),
            pltpu.VMEM((SOURCES, count, LAGS), jnp.float32),
            pltpu.SemaphoreType.DMA((parts, 2)),
            pltpu.SemaphoreType.DMA,
        ],
        compiler_params=pltpu.CompilerParams(vmem_limit_bytes=CORRELATE_VMEM),
        cost_estimate=pl.CostEstimate(flops=3 * 10**9, bytes_accessed=6 * 10**6, transcendentals=0),
        name="correlate",
    )(src, w0, w1, lag)


def chip_sum_body(mine_ref, core_ref, out_ref):
    out_ref[...] = (mine_ref[...] + core_ref[...]).astype(jnp.bfloat16)


def chip_sum(mine, core):
    return pl.pallas_call(
        chip_sum_body,
        in_specs=[pl.BlockSpec(memory_space=pltpu.VMEM)] * 2,
        out_specs=pl.BlockSpec(memory_space=pltpu.VMEM),
        out_shape=jax.ShapeDtypeStruct(mine.shape, jnp.bfloat16),
        compiler_params=pltpu.CompilerParams(vmem_limit_bytes=SUM_VMEM),
        cost_estimate=pl.CostEstimate(flops=10**5, bytes_accessed=10**6, transcendentals=0),
        name="chip_sum",
    )(mine, core)


def gather_sum_body(mine_ref, core_ref, far_ref, out_ref):
    total = (mine_ref[...] + core_ref[...]) + far_ref[...].astype(jnp.float32)
    for q in range(SOURCES):
        out_ref[:, q, :] = total[q]


def gather_sum(mine, core, far):
    shape = mine.shape
    return pl.pallas_call(
        gather_sum_body,
        in_specs=[pl.BlockSpec(memory_space=pltpu.VMEM)] * 3,
        out_specs=pl.BlockSpec(memory_space=pltpu.VMEM),
        out_shape=jax.ShapeDtypeStruct((shape[1], shape[0], shape[2]), jnp.float32),
        compiler_params=pltpu.CompilerParams(vmem_limit_bytes=SUM_VMEM),
        cost_estimate=pl.CostEstimate(flops=10**6, bytes_accessed=10**6, transcendentals=0),
        name="gather_sum",
    )(mine, core, far)


def local(raw, source_index, source_block):
    segs = raw.shape[0] * lax.axis_size("seg")
    ways = lax.axis_size("ch")
    table = jnp.asarray(dft_rows())
    lag = jnp.asarray(lag_rows(1.0 / (FREQS * segs)))
    picked = pick(raw, source_index, source_block)
    parts = lax.all_to_all(picked.reshape(ways, 8, SEGLEN), "ch", 0, 0)
    w0, done = whiten(raw, table, 0)
    spread = source_rows(parts, table, done)
    src = lax.all_to_all(spread, "ch", 0, 0)
    w1, _ = whiten(raw, table, 1)
    parts = correlate(src, w0, w1, lag)

    def swap(x, r):
        return lax.ppermute(x, "seg", [(i, i ^ r) for i in range(4)])

    far = swap(chip_sum(parts[2], swap(parts[3], 1)), 2)
    return gather_sum(parts[0], swap(parts[1], 1), far)


def solution(mesh):
    return jax.shard_map(
        local,
        mesh=mesh,
        in_specs=(P("seg", "ch", None), P(), P()),
        out_specs=P(("ch", "seg"), None, None),
        check_vma=False,
    )
```
